256 devices in a mesh: band: 32 (over z, x_hi, core), fft: 8 (over x_lo, y).
Axes of the slice: x: 4 (x_hi: 2, x_lo: 2; x = x_hi * 2 + x_lo), y: 4, z: 8, core: 2. Of those that a mesh axis runs over, the one named last changes fastest.
Arguments:
- orbitals: float32 [32, 128, 128, 128], P('band', 'fft'), may hold values from -1.2 to 1.2
Outputs:
- own_exchange: float32 [32, 128, 128, 128], P('band', 'fft')
- source_exchange: float32 [4, 128, 128, 128], P(None, 'fft', 'band')
The draws below stay inside these ranges and needn't reach their ends.
All inputs are finite; a program needn't handle non-finite values.
Results may differ from the reference program's by a relative error of at most 0.0003.
Values sent between devices are 32-bit elements; how exact they have to be, the bound alone decides.
A program may use at most 64 MiB of HBM per device.

```python
import jax
import jax.numpy as jnp
from jax import lax

N = 128
ROUNDS = 4
BANDS = 32


def draw_orbitals(key, part):
    key = jax.random.fold_in(key, 7)
    shape = (BANDS, N, N, N)
    return 0.5 * jax.random.truncated_normal(key, -2.4, 2.4, shape, jnp.float32)


def setup_inputs(seed: int = 0) -> dict:
    streams_of = jax.random.split(jax.random.key(seed), 2)
    return {
        "orbitals": draw_orbitals(jax.random.fold_in(streams_of[1], 71), 0),
    }


cell_length = 51.3


def signed_square(indices, grid_size):
    signed = jnp.where(indices <= grid_size // 2, indices, indices - grid_size)
    return (signed * signed).astype(jnp.float32)


def coulomb_kernel(first, count, grid_size):
    whole = jnp.arange(grid_size, dtype=jnp.int32)
    block = first + jnp.arange(count, dtype=jnp.int32)
    total = signed_square(whole, grid_size)[:, None, None] + signed_square(block, grid_size)[None, :, None] + signed_square(whole, grid_size)[None, None, :]
    scale = cell_length * cell_length / jnp.pi
    return jnp.where(total > 0, scale / jnp.maximum(total, 1.0), 0.0).astype(jnp.float32)


def reference(orbitals):
    bands = orbitals.shape[0]
    grid_size = orbitals.shape[1]
    stride = bands // ROUNDS
    sources = jnp.stack([orbitals[turn * stride] for turn in range(ROUNDS)])
    kernel = coulomb_kernel(0, grid_size, grid_size)

    def step(carry, orbital):
        pair = orbital[None] * sources
        spectrum = jnp.fft.fftn(pair, axes=(1, 2, 3))
        potential = jnp.real(jnp.fft.ifftn(spectrum * kernel[None], axes=(1, 2, 3))).astype(jnp.float32)
        own = jnp.sum(sources * potential, axis=0)
        return carry + orbital[None] * potential, own

    start = jnp.zeros((ROUNDS, grid_size, grid_size, grid_size), jnp.float32)
    source_exchange, own_exchange = lax.scan(step, start, orbitals)
    return own_exchange, source_exchange
```

```python
import functools

import jax
import jax.numpy as jnp
import ml_dtypes
import numpy as np
from jax import lax
from jax.experimental import pallas as pl
from jax.experimental.pallas import tpu as pltpu
from jax.sharding import PartitionSpec as P

N = 128
ROUNDS = 4
SLAB = 16
STEPS = 8
PACKS = 2
ZS = 8
CELL = 51.3
MESH = pl.DeviceIdType.MESH


def matrices():
    index = np.arange(N)
    angle = 2.0 * np.pi * (np.outer(index, index) % N) / N
    cosine, sine = np.cos(angle), np.sin(angle)
    forward = np.block([[cosine, -sine], [sine, cosine]])

    def split(matrix):
        high = matrix.astype(np.float32).astype(ml_dtypes.bfloat16)
        low = (matrix - high.astype(np.float64)).astype(np.float32).astype(ml_dtypes.bfloat16)
        return high, low

    def right(matrix):
        high, low = split(matrix)
        return np.concatenate([high, high, low], axis=0)

    def left(matrix):
        high, low = split(matrix)
        return np.concatenate([high, high, low], axis=1)

    return right(forward), left(forward.T), left(forward), right(forward.T)


def parts(value, axis):
    high = value.astype(jnp.bfloat16)
    low = (value - high.astype(jnp.float32)).astype(jnp.bfloat16)
    return jnp.concatenate([high, low, high], axis=axis)


def from_right(value, matrix):
    return jnp.dot(parts(value, 1), matrix, preferred_element_type=jnp.float32)


def from_left(matrix, value):
    return jnp.dot(matrix, parts(value, 0), preferred_element_type=jnp.float32)


def signed_square(index):
    signed = jnp.where(index <= N // 2, index, index - N)
    return (signed * signed).astype(jnp.float32)


def kernel(
    orb, right_fwd, left_fwd, left_inv, right_inv, own, out,
    srcs, send_a, recv_b, back, recv_c, terms, summed, gathered, coulomb, folded, folded_in, final, final_in,
    src_recv, src_send, a_recv, a_send, c_recv, c_send, t_recv, t_send, z_recv, z_send, x_sem, f_sem,
):
    band = lax.axis_index("band")
    me = lax.axis_index("fft")
    z = band // 4
    x_hi = lax.rem(band // 2, 2)
    core = lax.rem(band, 2)
    x_lo = me // 4
    y = lax.rem(me, 4)
    even = lax.rem(z, 2) == 0
    root = jnp.logical_and(jnp.logical_and(even, x_hi == 0), core == 0)
    lead = core == 0

    def device(z_at, x_hi_at, core_at):
        return {"band": z_at * 4 + x_hi_at * 2 + core_at, "fft": me}

    plus = device(lax.rem(z + 1, ZS), x_hi, core)
    minus = device(lax.rem(z + ZS - 1, ZS), x_hi, core)
    sibling = device(z, x_hi, 1 - core)
    across = device(z, 1 - x_hi, core)

    def peer_index(step):
        d_lo, d_y = step // 4, lax.rem(step, 4)
        return lax.rem(x_lo + d_lo, 2) * 4 + lax.rem(y + d_y, 4)

    barrier = pltpu.get_barrier_semaphore()

    def signal(target):
        pl.semaphore_signal(barrier, inc=1, device_id=target, device_id_type=MESH)

    for step in range(1, 8):
        signal({"band": band, "fft": peer_index(step)})
    for step in range(1, ZS):
        signal(device(lax.rem(z + step, ZS), x_hi, core))
    signal(sibling)
    signal(across)
    pl.semaphore_wait(barrier, 16)

    def round_of(slot):
        return lax.rem(z // 2 + slot, ROUNDS)

    def planes(j):
        return pl.ds(2 * j, 2)

    def remote(src, dst, send_sem, recv_sem, target):
        return pltpu.make_async_remote_copy(
            src_ref=src, dst_ref=dst, send_sem=send_sem, recv_sem=recv_sem, device_id=target, device_id_type=MESH
        )

    def pass_on(src, slot, j, kind, target):
        r = round_of(slot)
        remote(src, srcs.at[r, planes(j)], src_send.at[slot, kind], src_recv.at[r, j], target).start()

    @pl.when(root)
    def _():
        def body(j, carry):
            chunk = orb.at[planes(j)]
            pass_on(chunk, 0, j, 0, plus)
            pass_on(chunk, 0, j, 1, minus)
            pass_on(chunk, 0, j, 2, sibling)
            pass_on(chunk, 0, j, 3, across)
            return carry

        lax.fori_loop(0, STEPS, body, 0)

        def fill(j, carry):
            srcs[round_of(0), planes(j)] = orb[planes(j)]
            return carry

        lax.fori_loop(0, STEPS, fill, 0)

    def arrive(slot, j):
        r = round_of(slot)
        chunk = srcs.at[r, planes(j)]

        def take():
            pltpu.make_async_copy(chunk, chunk, src_recv.at[r, j]).wait()

            @pl.when(lead)
            def _():
                if slot in (0, 3):
                    pass_on(chunk, slot, j, 0, plus)
                if slot == 1:
                    pass_on(chunk, slot, j, 1, minus)
                if slot == 0:

                    @pl.when(even)
                    def _():
                        pass_on(chunk, slot, j, 1, minus)

                pass_on(chunk, slot, j, 2, sibling)

        if slot == 0:
            pl.when(jnp.logical_not(root))(take)
        else:
            take()

    def fill_coulomb(k, carry):
        row = lax.broadcasted_iota(jnp.int32, (N, N), 0)
        column = lax.broadcasted_iota(jnp.int32, (N, N), 1)
        middle = jnp.full((N, N), me * SLAB + k, jnp.int32)
        total = signed_square(row) + signed_square(middle) + signed_square(column)
        scale = CELL * CELL / np.pi / float(N) ** 3
        coulomb[k] = jnp.where(total > 0, scale / jnp.maximum(total, 1.0), 0.0)
        return carry

    lax.fori_loop(0, SLAB, fill_coulomb, 0)

    def forward(p, j):
        r_a, r_b = round_of(2 * p), round_of(2 * p + 1)
        rows = []
        for i in range(2):
            o = orb[2 * j + i]
            rows.append(jnp.concatenate([o * srcs[r_a, 2 * j + i], o * srcs[r_b, 2 * j + i]], axis=1))
        along_z = from_right(jnp.concatenate(rows, axis=0), right_fwd[...])
        real = jnp.concatenate([along_z[:N, :N], along_z[N:, :N]], axis=1)
        imag = jnp.concatenate([along_z[:N, N:], along_z[N:, N:]], axis=1)
        along_y = from_left(left_fwd[...], jnp.concatenate([real, imag], axis=0))
        for i in range(2):
            for part in range(2):
                send_a[p, 2 * j + i, part] = along_y[part * N : (part + 1) * N, i * N : (i + 1) * N]
        place = pl.ds(me * SLAB + 2 * j, 2)

        def block(f):
            return send_a.at[p, planes(j), :, pl.ds(pl.multiple_of(f * SLAB, SLAB), SLAB), :]

        for step in (5, 7, 6, 1, 3, 2, 4):
            f = peer_index(step)
            remote(
                block(f), recv_b.at[p, place], a_send.at[p], a_recv.at[p], {"band": band, "fft": f}
            ).start()
        pltpu.make_async_copy(block(me), recv_b.at[p, place], a_recv.at[p]).start()

    def first_steps(j, carry):
        arrive(0, j)
        arrive(1, j)
        forward(0, j)
        arrive(3, j)
        arrive(2, j)
        return carry

    def second_steps(j, carry):
        forward(1, j)
        return carry

    lax.fori_loop(0, STEPS, first_steps, 0)
    lax.fori_loop(0, STEPS, second_steps, 0)

    def middle(p):
        pltpu.make_async_copy(recv_b.at[p], recv_b.at[p], a_recv.at[p]).wait()
        flat_in = recv_b.at[p].reshape(N * 2 * SLAB, N)
        flat_out = back.at[p].reshape(N * 2 * SLAB, N)

        def rows(part, k):
            return pl.ds(part * SLAB + k, N, stride=2 * SLAB)

        def body(i, carry):
            blocks = [
                jnp.concatenate([flat_in[rows(part, 2 * i), :], flat_in[rows(part, 2 * i + 1), :]], axis=1)
                for part in range(2)
            ]
            spectrum = from_left(left_fwd[...], jnp.concatenate(blocks, axis=0))
            weight = jnp.concatenate([coulomb[2 * i], coulomb[2 * i + 1]], axis=1)
            spectrum = spectrum * jnp.concatenate([weight, weight], axis=0)
            result = from_left(left_inv[...], spectrum)
            for part in range(2):
                for n in range(2):
                    flat_out[rows(part, 2 * i + n), :] = result[part * N : (part + 1) * N, n * N : (n + 1) * N]
            return carry

        lax.fori_loop(0, SLAB // 2, body, 0)

        def give(j, carry):
            def place(ref):
                return ref.at[p, planes(j), :, pl.ds(pl.multiple_of(me * SLAB, SLAB), SLAB), :]

            for step in (5, 7, 6, 1, 3, 2, 4):
                f = peer_index(step)
                remote(
                    back.at[p, pl.ds(f * SLAB + 2 * j, 2)], place(recv_c), c_send.at[p], c_recv.at[p, j],
                    {"band": band, "fft": f},
                ).start()
            pltpu.make_async_copy(
                back.at[p, pl.ds(me * SLAB + 2 * j, 2)], place(recv_c), c_recv.at[p, j]
            ).start()
            return carry

        lax.fori_loop(0, STEPS, give, 0)

    for p in range(PACKS):
        middle(p)

    def inverse(p, j):
        chunk = recv_c.at[p, planes(j)]
        pltpu.make_async_copy(chunk, chunk, c_recv.at[p, j]).wait()
        parts_in = [
            jnp.concatenate([recv_c[p, 2 * j, part], recv_c[p, 2 * j + 1, part]], axis=1) for part in range(2)
        ]
        along_y = from_left(left_inv[...], jnp.concatenate(parts_in, axis=0))
        rows = [
            jnp.concatenate([along_y[:N, i * N : (i + 1) * N], along_y[N:, i * N : (i + 1) * N]], axis=1)
            for i in range(2)
        ]
        potential = from_right(jnp.concatenate(rows, axis=0), right_inv[...])
        r_a, r_b = round_of(2 * p), round_of(2 * p + 1)
        for i in range(2):
            pot_a = potential[i * N : (i + 1) * N, :N]
            pot_b = potential[i * N : (i + 1) * N, N:]
            share = srcs[r_a, 2 * j + i] * pot_a + srcs[r_b, 2 * j + i] * pot_b
            if p > 0:
                share = own[2 * j + i] + share
            own[2 * j + i] = share
            o = orb[2 * j + i]
            terms[p, j, i, 0] = o * pot_a
            terms[p, j, i, 1] = o * pot_b
        remote(
            terms.at[p, j, 1 - core], summed.at[p, j], t_send.at[p], t_recv.at[p, j], sibling
        ).start()

    def spread(p, j):
        chunk = summed.at[p, j]
        pltpu.make_async_copy(chunk, chunk, t_recv.at[p, j]).wait()
        summed[p, j] = summed[p, j] + terms[p, j, core]

        def rows(z_at):
            return summed.at[p, j, :, pl.ds(pl.multiple_of(z_at * 16, 16), 16), :]

        for step in (4, 3, 5, 2, 6, 1, 7):
            z_at = lax.rem(z + step, ZS)
            remote(
                rows(z_at), gathered.at[z, pl.ds(2 * p, 2), j], z_send.at[p], z_recv.at[0], device(z_at, x_hi, core)
            ).start()
        gathered[z, pl.ds(2 * p, 2), j] = summed[p, j, :, pl.ds(pl.multiple_of(z * 16, 16), 16), :]

    for p in range(PACKS):

        def step_body(j, carry):
            inverse(p, j)

            @pl.when(j > 0)
            def _():
                spread(p, j - 1)

            return carry

        lax.fori_loop(0, STEPS, step_body, 0)
        spread(p, STEPS - 1)

    pltpu.make_async_copy(gathered.at[pl.ds(0, 7)], gathered.at[pl.ds(0, 7)], z_recv.at[0]).wait()
    for r in range(ROUNDS):
        total = gathered[0, r]
        for z_at in range(1, ZS):
            total = total + gathered[z_at, (r - z_at // 2) % ROUNDS]
        folded[r] = total

    def half(x_hi_at):
        return pl.ds(pl.multiple_of(x_hi_at * 8, 8), 8)

    cross = remote(folded.at[:, :, half(1 - x_hi), :], folded_in, x_sem.at[0], x_sem.at[1], across)
    cross.start()
    cross.wait()
    final[...] = folded[:, :, half(x_hi), :] + folded_in[...]
    last = remote(final, final_in, f_sem.at[0], f_sem.at[1], sibling)
    last.start()
    last.wait()

    def write(j, carry):
        for r in range(ROUNDS):
            mine, theirs = final[r, j], final_in[r, j]
            out[r, 2 * j + core] = jnp.where(core == 0, mine[:4], mine[4:])
            out[r, 2 * j + 1 - core] = jnp.where(core == 0, theirs[:4], theirs[4:])
        return carry

    lax.fori_loop(0, STEPS, write, 0)

    def sent(ref, sem):
        pltpu.make_async_copy(ref, ref, sem).wait()

    for p in range(PACKS):
        sent(send_a.at[p, pl.ds(0, 14)], a_send.at[p])
        sent(back.at[p, pl.ds(0, 112)], c_send.at[p])
        sent(summed.at[p], t_send.at[p])
        sent(summed.at[p, pl.ds(0, 7)], z_send.at[p])

    @pl.when(lead)
    def _():
        for slot, kind in ((0, 0), (0, 2), (1, 1), (1, 2), (2, 2), (3, 0), (3, 2)):
            sent(srcs.at[slot], src_send.at[slot, kind])

        @pl.when(even)
        def _():
            sent(srcs.at[0], src_send.at[0, 1])

        @pl.when(root)
        def _():
            sent(srcs.at[0], src_send.at[0, 3])


def local(right_fwd, left_fwd, left_inv, right_inv, orbitals):
    f32 = jnp.float32
    dma = pltpu.SemaphoreType.DMA
    vmem = pl.BlockSpec(memory_space=pltpu.VMEM)
    own, source = pl.pallas_call(
        kernel,
        out_shape=(
            jax.ShapeDtypeStruct((SLAB, N, N), f32),
            jax.ShapeDtypeStruct((ROUNDS, SLAB, 4, N), f32),
        ),
        in_specs=[vmem] * 5,
        out_specs=(vmem, vmem),
        scratch_shapes=[
            pltpu.VMEM((ROUNDS, SLAB, N, N), f32),
            pltpu.VMEM((PACKS, SLAB, 2, N, N), f32),
            pltpu.VMEM((PACKS, N, 2, SLAB, N), f32),
            pltpu.VMEM((PACKS, N, 2, SLAB, N), f32),
            pltpu.VMEM((PACKS, SLAB, 2, N, N), f32),
            pltpu.VMEM((PACKS, STEPS, 2, 2, N, N), f32),
            pltpu.VMEM((PACKS, STEPS, 2, N, N), f32),
            pltpu.VMEM((ZS, ROUNDS, STEPS, 16, N), f32),
            pltpu.VMEM((SLAB, N, N), f32),
            pltpu.VMEM((ROUNDS, STEPS, 16, N), f32),
            pltpu.VMEM((ROUNDS, STEPS, 8, N), f32),
            pltpu.VMEM((ROUNDS, STEPS, 8, N), f32),
            pltpu.VMEM((ROUNDS, STEPS, 8, N), f32),
            dma((ROUNDS, STEPS)),
            dma((ROUNDS, 4)),
            dma((PACKS,)),
            dma((PACKS,)),
            dma((PACKS, STEPS)),
            dma((PACKS,)),
            dma((PACKS, STEPS)),
            dma((PACKS,)),
            dma((1,)),
            dma((PACKS,)),
            dma((2,)),
            dma((2,)),
        ],
        compiler_params=pltpu.CompilerParams(
            collective_id=0, has_side_effects=True, vmem_limit_bytes=48 * 2**20
        ),
        name="exchange",
    )(orbitals[0], right_fwd, left_fwd, left_inv, right_inv)
    return own[None], source


def solution(mesh):
    tables = [jnp.asarray(table) for table in matrices()]
    in_specs = (P("band", "fft", None, None),)
    out_specs = (P("band", "fft", None, None), P(None, "fft", "band", None))
    body = functools.partial(local, *tables)
    return jax.shard_map(body, mesh=mesh, in_specs=in_specs, out_specs=out_specs, check_vma=False)
```

```python
import functools

import jax
import jax.numpy as jnp
import ml_dtypes
import numpy as np
from jax import lax
from jax.experimental import pallas as pl
from jax.experimental.pallas import tpu as pltpu
from jax.sharding import PartitionSpec as P

N = 128
ROUNDS = 4
SLAB = 16
STEPS = 8
PACKS = 2
ZS = 8
CELL = 51.3
LAG = 4
MESH = pl.DeviceIdType.MESH


def matrices():
    index = np.arange(N)
    angle = 2.0 * np.pi * (np.outer(index, index) % N) / N
    cosine, sine = np.cos(angle), np.sin(angle)
    forward = np.block([[cosine, -sine], [sine, cosine]])

    def split(matrix):
        high = matrix.astype(np.float32).astype(ml_dtypes.bfloat16)
        low = (matrix - high.astype(np.float64)).astype(np.float32).astype(ml_dtypes.bfloat16)
        return high, low

    def right(matrix):
        high, low = split(matrix)
        return np.concatenate([high, high, low], axis=0)

    def left(matrix):
        high, low = split(matrix)
        return np.concatenate([high, high, low], axis=1)

    return np.stack([right(forward), right(forward.T)]), np.stack([left(forward.T), left(forward)])


def parts(value, axis):
    high = value.astype(jnp.bfloat16)
    low = (value - high.astype(jnp.float32)).astype(jnp.bfloat16)
    return jnp.concatenate([high, low, high], axis=axis)


def from_right(value, matrix):
    return jnp.dot(parts(value, 1), matrix, preferred_element_type=jnp.float32)


def from_left(matrix, value):
    return jnp.dot(matrix, parts(value, 0), preferred_element_type=jnp.float32)


def signed_square(index):
    signed = jnp.where(index <= N // 2, index, index - N)
    return (signed * signed).astype(jnp.float32)


def kernel(
    orb_in, rights_in, lefts_in, own, out,
    orb, rights, lefts, srcs, send_a, recv_b, back, recv_c, terms, summed, gathered, coulomb, folded, folded_in, final, final_in,
    in_sem, src_recv, src_send, a_recv, a_send, c_recv, c_send, t_recv, t_send, z_recv, z_send, x_recv, x_send, f_recv, f_send,
):
    band = lax.axis_index("band")
    me = lax.axis_index("fft")
    z = band // 4
    x_hi = lax.rem(band // 2, 2)
    core = lax.rem(band, 2)
    x_lo = me // 4
    y = lax.rem(me, 4)
    even = lax.rem(z, 2) == 0
    root = jnp.logical_and(jnp.logical_and(even, x_hi == 0), core == 0)
    lead = core == 0

    loads = [
        pltpu.make_async_copy(src, dst, in_sem.at[i])
        for i, (src, dst) in enumerate(((orb_in, orb), (rights_in, rights), (lefts_in, lefts)))
    ]
    for load in loads:
        load.start()

    def device(z_at, x_hi_at, core_at):
        return {"band": z_at * 4 + x_hi_at * 2 + core_at, "fft": me}

    plus = device(lax.rem(z + 1, ZS), x_hi, core)
    minus = device(lax.rem(z + ZS - 1, ZS), x_hi, core)
    sibling = device(z, x_hi, 1 - core)
    across = device(z, 1 - x_hi, core)

    def peer_index(step):
        d_lo, d_y = step // 4, lax.rem(step, 4)
        return lax.rem(x_lo + d_lo, 2) * 4 + lax.rem(y + d_y, 4)

    barrier = pltpu.get_barrier_semaphore()

    def signal(target):
        pl.semaphore_signal(barrier, inc=1, device_id=target, device_id_type=MESH)

    for step in range(1, 8):
        signal({"band": band, "fft": peer_index(step)})
    for step in range(1, ZS):
        signal(device(lax.rem(z + step, ZS), x_hi, core))
    signal(sibling)
    signal(across)
    loads[0].wait()
    pl.semaphore_wait(barrier, 16)

    def round_of(slot):
        return lax.rem(z // 2 + slot, ROUNDS)

    def planes(j):
        return pl.ds(2 * j, 2)

    def remote(src, dst, send_sem, recv_sem, target):
        return pltpu.make_async_remote_copy(
            src_ref=src, dst_ref=dst, send_sem=send_sem, recv_sem=recv_sem, device_id=target, device_id_type=MESH
        )

    def pass_on(src, slot, j, kind, target):
        r = round_of(slot)
        remote(src, srcs.at[r, planes(j)], src_send.at[slot, kind], src_recv.at[r, j], target).start()

    @pl.when(root)
    def _():
        def body(j, carry):
            chunk = orb.at[planes(j)]
            pass_on(chunk, 0, j, 0, plus)
            pass_on(chunk, 0, j, 1, minus)
            pass_on(chunk, 0, j, 2, sibling)
            pass_on(chunk, 0, j, 3, across)
            return carry

        lax.fori_loop(0, STEPS, body, 0)

        def fill(j, carry):
            srcs[round_of(0), planes(j)] = orb[planes(j)]
            return carry

        lax.fori_loop(0, STEPS, fill, 0)

    def arrive(slot, j):
        r = round_of(slot)
        chunk = srcs.at[r, planes(j)]

        def take():
            pltpu.make_async_copy(chunk, chunk, src_recv.at[r, j]).wait()

            @pl.when(lead)
            def _():
                if slot in (0, 3):
                    pass_on(chunk, slot, j, 0, plus)
                if slot == 1:
                    pass_on(chunk, slot, j, 1, minus)
                if slot == 0:

                    @pl.when(even)
                    def _():
                        pass_on(chunk, slot, j, 1, minus)

                pass_on(chunk, slot, j, 2, sibling)

        if slot == 0:
            pl.when(jnp.logical_not(root))(take)
        else:
            take()

    def fill_coulomb(k, carry):
        row = lax.broadcasted_iota(jnp.int32, (N, N), 0)
        column = lax.broadcasted_iota(jnp.int32, (N, N), 1)
        middle = jnp.full((N, N), me * SLAB + k, jnp.int32)
        total = signed_square(row) + signed_square(middle) + signed_square(column)
        scale = CELL * CELL / np.pi / float(N) ** 3
        coulomb[k] = jnp.where(total > 0, scale / jnp.maximum(total, 1.0), 0.0)
        return carry

    lax.fori_loop(0, SLAB, fill_coulomb, 0)
    for load in loads[1:]:
        load.wait()

    def forward(p, j):
        r_a, r_b = round_of(2 * p), round_of(2 * p + 1)
        rows = []
        for i in range(2):
            o = orb[2 * j + i]
            rows.append(jnp.concatenate([o * srcs[r_a, 2 * j + i], o * srcs[r_b, 2 * j + i]], axis=1))
        along_z = from_right(jnp.concatenate(rows, axis=0), rights[0])
        real = jnp.concatenate([along_z[:N, :N], along_z[N:, :N]], axis=1)
        imag = jnp.concatenate([along_z[:N, N:], along_z[N:, N:]], axis=1)
        along_y = from_left(lefts[0], jnp.concatenate([real, imag], axis=0))
        for i in range(2):
            for part in range(2):
                send_a[p, 2 * j + i, part] = along_y[part * N : (part + 1) * N, i * N : (i + 1) * N]
        place = pl.ds(me * SLAB + 2 * j, 2)

        def block(f):
            return send_a.at[p, planes(j), :, pl.ds(pl.multiple_of(f * SLAB, SLAB), SLAB), :]

        for step in (5, 7, 6, 1, 3, 2, 4):
            f = peer_index(step)
            remote(
                block(f), recv_b.at[p, place], a_send.at[p], a_recv.at[p], {"band": band, "fft": f}
            ).start()
        pltpu.make_async_copy(block(me), recv_b.at[p, place], a_recv.at[p]).start()

    behind = {0: 0, 1: jnp.where(even, LAG, 1), 3: jnp.where(even, 6, 9), 2: jnp.where(even, 12, 9)}

    def relay(i):
        for slot in (0, 1, 3, 2):
            j = i - behind[slot]

            @pl.when(jnp.logical_and(j >= 0, j < STEPS))
            def _():
                arrive(slot, j)

    def first_steps(i, carry):
        relay(i)

        @pl.when(i >= LAG)
        def _():
            forward(0, i - LAG)

        return carry

    def second_steps(i, carry):
        relay(i)
        forward(1, i - STEPS - LAG)
        return carry

    lax.fori_loop(0, STEPS + LAG, first_steps, 0)
    lax.fori_loop(STEPS + LAG, 2 * STEPS + LAG, second_steps, 0)

    def middle(p):
        pltpu.make_async_copy(recv_b.at[p], recv_b.at[p], a_recv.at[p]).wait()
        flat_in = recv_b.at[p].reshape(N * 2 * SLAB, N)
        flat_out = back.at[p].reshape(N * 2 * SLAB, N)

        def rows(part, k):
            return pl.ds(part * SLAB + k, N, stride=2 * SLAB)

        def body(i, carry):
            blocks = [
                jnp.concatenate([flat_in[rows(part, 2 * i), :], flat_in[rows(part, 2 * i + 1), :]], axis=1)
                for part in range(2)
            ]
            spectrum = from_left(lefts[0], jnp.concatenate(blocks, axis=0))
            weight = jnp.concatenate([coulomb[2 * i], coulomb[2 * i + 1]], axis=1)
            spectrum = spectrum * jnp.concatenate([weight, weight], axis=0)
            result = from_left(lefts[1], spectrum)
            for part in range(2):
                for n in range(2):
                    flat_out[rows(part, 2 * i + n), :] = result[part * N : (part + 1) * N, n * N : (n + 1) * N]
            return carry

        lax.fori_loop(0, SLAB // 2, body, 0)

        def give(j, carry):
            def place(ref):
                return ref.at[p, planes(j), :, pl.ds(pl.multiple_of(me * SLAB, SLAB), SLAB), :]

            for step in (5, 7, 6, 1, 3, 2, 4):
                f = peer_index(step)
                remote(
                    back.at[p, pl.ds(f * SLAB + 2 * j, 2)], place(recv_c), c_send.at[p], c_recv.at[p, j],
                    {"band": band, "fft": f},
                ).start()
            pltpu.make_async_copy(
                back.at[p, pl.ds(me * SLAB + 2 * j, 2)], place(recv_c), c_recv.at[p, j]
            ).start()
            return carry

        lax.fori_loop(0, STEPS, give, 0)

    for p in range(PACKS):
        middle(p)

    def inverse(p, j):
        chunk = recv_c.at[p, planes(j)]
        pltpu.make_async_copy(chunk, chunk, c_recv.at[p, j]).wait()
        parts_in = [
            jnp.concatenate([recv_c[p, 2 * j, part], recv_c[p, 2 * j + 1, part]], axis=1) for part in range(2)
        ]
        along_y = from_left(lefts[1], jnp.concatenate(parts_in, axis=0))
        rows = [
            jnp.concatenate([along_y[:N, i * N : (i + 1) * N], along_y[N:, i * N : (i + 1) * N]], axis=1)
            for i in range(2)
        ]
        potential = from_right(jnp.concatenate(rows, axis=0), rights[1])
        r_a, r_b = round_of(2 * p), round_of(2 * p + 1)
        for i in range(2):
            pot_a = potential[i * N : (i + 1) * N, :N]
            pot_b = potential[i * N : (i + 1) * N, N:]
            share = srcs[r_a, 2 * j + i] * pot_a + srcs[r_b, 2 * j + i] * pot_b
            if p > 0:
                share = own[2 * j + i] + share
            own[2 * j + i] = share
            o = orb[2 * j + i]
            terms[p, j, i, 0] = o * pot_a
            terms[p, j, i, 1] = o * pot_b
        remote(
            terms.at[p, j, 1 - core], summed.at[p, j], t_send.at[p], t_recv.at[p, j], sibling
        ).start()

    def spread(p, j):
        chunk = summed.at[p, j]
        pltpu.make_async_copy(chunk, chunk, t_recv.at[p, j]).wait()
        summed[p, j] = summed[p, j] + terms[p, j, core]

        def rows(z_at):
            return summed.at[p, j, :, pl.ds(pl.multiple_of(z_at * 16, 16), 16), :]

        for step in (4, 3, 5, 2, 6, 1, 7):
            z_at = lax.rem(z + step, ZS)
            remote(
                rows(z_at), gathered.at[z, pl.ds(2 * p, 2), j], z_send.at[p], z_recv.at[j], device(z_at, x_hi, core)
            ).start()
        gathered[z, pl.ds(2 * p, 2), j] = summed[p, j, :, pl.ds(pl.multiple_of(z * 16, 16), 16), :]

    def half(x_hi_at):
        return pl.ds(pl.multiple_of(x_hi_at * 8, 8), 8)

    def cross(j):
        return remote(
            folded.at[j, :, half(1 - x_hi), :], folded_in.at[j], x_send.at[0], x_recv.at[j], across
        )

    def last(j):
        return remote(final.at[j], final_in.at[j], f_send.at[0], f_recv.at[j], sibling)

    def fold(j):
        arrived = gathered.at[pl.ds(0, 7), :, j]
        pltpu.make_async_copy(arrived, arrived, z_recv.at[j]).wait()
        for r in range(ROUNDS):
            total = gathered[0, r, j]
            for z_at in range(1, ZS):
                total = total + gathered[z_at, (r - z_at // 2) % ROUNDS, j]
            folded[j, r] = total
        cross(j).start()

    def finish(j):
        cross(j).wait_recv()
        final[j] = folded[j, :, half(x_hi), :] + folded_in[j]
        last(j).start()

    def write(j):
        last(j).wait_recv()
        for r in range(ROUNDS):
            mine, theirs = final[j, r], final_in[j, r]
            out[r, 2 * j + core] = jnp.where(core == 0, mine[:4], mine[4:])
            out[r, 2 * j + 1 - core] = jnp.where(core == 0, theirs[:4], theirs[4:])

    def second_half(p, stages, i, carry):
        for late, stage in stages:
            j = i - late

            @pl.when(jnp.logical_and(j >= 0, j < STEPS))
            def _():
                stage(j)

        return carry

    for p in range(PACKS):
        stages = [(0, functools.partial(inverse, p)), (1, functools.partial(spread, p))]
        if p == PACKS - 1:
            stages += [(3, fold), (4, finish), (5, write)]
        lax.fori_loop(0, STEPS + stages[-1][0], functools.partial(second_half, p, stages), 0)

    def sent(ref, sem):
        pltpu.make_async_copy(ref, ref, sem).wait()

    for p in range(PACKS):
        sent(send_a.at[p, pl.ds(0, 14)], a_send.at[p])
        sent(back.at[p, pl.ds(0, 112)], c_send.at[p])
        sent(summed.at[p], t_send.at[p])
        sent(summed.at[p, pl.ds(0, 7)], z_send.at[p])
    sent(folded_in, x_send.at[0])
    sent(final, f_send.at[0])

    @pl.when(lead)
    def _():
        for slot, kind in ((0, 0), (0, 2), (1, 1), (1, 2), (2, 2), (3, 0), (3, 2)):
            sent(srcs.at[slot], src_send.at[slot, kind])

        @pl.when(even)
        def _():
            sent(srcs.at[0], src_send.at[0, 1])

        @pl.when(root)
        def _():
            sent(srcs.at[0], src_send.at[0, 3])


def local(rights, lefts, orbitals):
    f32 = jnp.float32
    dma = pltpu.SemaphoreType.DMA
    vmem = pl.BlockSpec(memory_space=pltpu.VMEM)
    own, source = pl.pallas_call(
        kernel,
        out_shape=(
            jax.ShapeDtypeStruct((SLAB, N, N), f32),
            jax.ShapeDtypeStruct((ROUNDS, SLAB, 4, N), f32),
        ),
        in_specs=[pl.BlockSpec(memory_space=pltpu.HBM)] * 3,
        out_specs=(vmem, vmem),
        scratch_shapes=[
            pltpu.VMEM((SLAB, N, N), f32),
            pltpu.VMEM(rights.shape, rights.dtype),
            pltpu.VMEM(lefts.shape, lefts.dtype),
            pltpu.VMEM((ROUNDS, SLAB, N, N), f32),
            pltpu.VMEM((PACKS, SLAB, 2, N, N), f32),
            pltpu.VMEM((PACKS, N, 2, SLAB, N), f32),
            pltpu.VMEM((PACKS, N, 2, SLAB, N), f32),
            pltpu.VMEM((PACKS, SLAB, 2, N, N), f32),
            pltpu.VMEM((PACKS, STEPS, 2, 2, N, N), f32),
            pltpu.VMEM((PACKS, STEPS, 2, N, N), f32),
            pltpu.VMEM((ZS, ROUNDS, STEPS, 16, N), f32),
            pltpu.VMEM((SLAB, N, N), f32),
            pltpu.VMEM((STEPS, ROUNDS, 16, N), f32),
            pltpu.VMEM((STEPS, ROUNDS, 8, N), f32),
            pltpu.VMEM((STEPS, ROUNDS, 8, N), f32),
            pltpu.VMEM((STEPS, ROUNDS, 8, N), f32),
            dma((3,)),
            dma((ROUNDS, STEPS)),
            dma((ROUNDS, 4)),
            dma((PACKS,)),
            dma((PACKS,)),
            dma((PACKS, STEPS)),
            dma((PACKS,)),
            dma((PACKS, STEPS)),
            dma((PACKS,)),
            dma((STEPS,)),
            dma((PACKS,)),
            dma((STEPS,)),
            dma((1,)),
            dma((STEPS,)),
            dma((1,)),
        ],
        compiler_params=pltpu.CompilerParams(
            collective_id=0, has_side_effects=True, vmem_limit_bytes=56 * 2**20
        ),
        name="exchange",
    )(orbitals[0], rights, lefts)
    return own[None], source


def solution(mesh):
    tables = [jnp.asarray(table) for table in matrices()]
    in_specs = (P("band", "fft", None, None),)
    out_specs = (P("band", "fft", None, None), P(None, "fft", "band", None))
    body = functools.partial(local, *tables)
    return jax.shard_map(body, mesh=mesh, in_specs=in_specs, out_specs=out_specs, check_vma=False)
```

```python
import functools

import jax
import jax.numpy as jnp
import ml_dtypes
import numpy as np
from jax import lax
from jax.experimental import pallas as pl
from jax.experimental.pallas import tpu as pltpu
from jax.sharding import PartitionSpec as P

N = 128
ROUNDS = 4
SLAB = 16
STEPS = 8
PACKS = 2
ZS = 8
CELL = 51.3
LAG = 3
EARLY = 4
AHEAD = 3
MESH = pl.DeviceIdType.MESH


def matrices():
    index = np.arange(N)
    angle = 2.0 * np.pi * (np.outer(index, index) % N) / N
    cosine, sine = np.cos(angle), np.sin(angle)
    forward = np.block([[cosine, -sine], [sine, cosine]])

    def split(matrix):
        high = matrix.astype(np.float32).astype(ml_dtypes.bfloat16)
        low = (matrix - high.astype(np.float64)).astype(np.float32).astype(ml_dtypes.bfloat16)
        return high, low

    def right(matrix):
        high, low = split(matrix)
        return np.concatenate([high, high, low], axis=0)

    def left(matrix):
        high, low = split(matrix)
        return np.concatenate([high, high, low], axis=1)

    return np.stack([right(forward), right(forward.T)]), np.stack([left(forward.T), left(forward)])


def parts(value, axis):
    high = value.astype(jnp.bfloat16)
    low = (value - high.astype(jnp.float32)).astype(jnp.bfloat16)
    return jnp.concatenate([high, low, high], axis=axis)


def from_right(value, matrix):
    return jnp.dot(parts(value, 1), matrix, preferred_element_type=jnp.float32)


def from_left(matrix, value):
    return jnp.dot(matrix, parts(value, 0), preferred_element_type=jnp.float32)


def signed_square(index):
    signed = jnp.where(index <= N // 2, index, index - N)
    return (signed * signed).astype(jnp.float32)


def kernel(
    orb_in, rights_in, lefts_in, own, out,
    orb, rights, lefts, srcs, send_a, recv_b, back, recv_c, terms, summed, gathered, coulomb, folded, folded_in,
    in_sem, src_recv, src_send, a_recv, a_send, c_recv, c_send, t_recv, t_send, z_recv, z_send, x_recv, x_send,
):
    band = lax.axis_index("band")
    me = lax.axis_index("fft")
    z = band // 4
    x_hi = lax.rem(band // 2, 2)
    core = lax.rem(band, 2)
    x_lo = me // 4
    y = lax.rem(me, 4)
    even = lax.rem(z, 2) == 0
    root = jnp.logical_and(jnp.logical_and(even, x_hi == 0), core == 0)
    lead = core == 0

    loads = [
        pltpu.make_async_copy(src, dst, in_sem.at[i])
        for i, (src, dst) in enumerate(((orb_in, orb), (rights_in, rights), (lefts_in, lefts)))
    ]
    for load in loads:
        load.start()

    def device(z_at, x_hi_at, core_at):
        return {"band": z_at * 4 + x_hi_at * 2 + core_at, "fft": me}

    plus = device(lax.rem(z + 1, ZS), x_hi, core)
    minus = device(lax.rem(z + ZS - 1, ZS), x_hi, core)
    minus2 = device(lax.rem(z + ZS - 2, ZS), x_hi, core)
    sibling = device(z, x_hi, 1 - core)
    across = device(z, 1 - x_hi, core)

    def peer_index(step):
        d_lo, d_y = step // 4, lax.rem(step, 4)
        return lax.rem(x_lo + d_lo, 2) * 4 + lax.rem(y + d_y, 4)

    barrier = pltpu.get_barrier_semaphore()

    def signal(target):
        pl.semaphore_signal(barrier, inc=1, device_id=target, device_id_type=MESH)

    for step in range(1, 8):
        signal({"band": band, "fft": peer_index(step)})
    for step in range(1, ZS):
        signal(device(lax.rem(z + step, ZS), x_hi, core))
    signal(sibling)
    signal(across)
    signal(device(z, 1 - x_hi, 1 - core))
    loads[0].wait()
    pl.semaphore_wait(barrier, 17)

    def round_of(slot):
        return lax.rem(z // 2 + slot, ROUNDS)

    def planes(j):
        return pl.ds(2 * j, 2)

    def remote(src, dst, send_sem, recv_sem, target):
        return pltpu.make_async_remote_copy(
            src_ref=src, dst_ref=dst, send_sem=send_sem, recv_sem=recv_sem, device_id=target, device_id_type=MESH
        )

    def pass_on(src, slot, j, kind, target):
        r = round_of(slot)
        remote(src, srcs.at[r, planes(j)], src_send.at[slot, kind], src_recv.at[r, j], target).start()

    def pass_early(chunk, j):
        @pl.when(j < EARLY)
        def _():
            pass_on(chunk, 0, j, 4, minus2)

    @pl.when(root)
    def _():
        def body(j, carry):
            chunk = orb.at[planes(j)]
            pass_on(chunk, 0, j, 3, across)
            pass_early(chunk, j)
            pass_on(chunk, 0, j, 1, minus)
            pass_on(chunk, 0, j, 0, plus)
            pass_on(chunk, 0, j, 2, sibling)
            return carry

        lax.fori_loop(0, STEPS, body, 0)

        def fill(j, carry):
            srcs[round_of(0), planes(j)] = orb[planes(j)]
            return carry

        lax.fori_loop(0, STEPS, fill, 0)

    def arrive(slot, j):
        r = round_of(slot)
        chunk = srcs.at[r, planes(j)]

        def take():
            pltpu.make_async_copy(chunk, chunk, src_recv.at[r, j]).wait()

            @pl.when(lead)
            def _():
                if slot == 1:

                    @pl.when(jnp.logical_or(even, j >= EARLY))
                    def _():
                        pass_on(chunk, slot, j, 1, minus)

                if slot == 0:

                    @pl.when(even)
                    def _():
                        pass_early(chunk, j)
                        pass_on(chunk, slot, j, 1, minus)

                if slot in (0, 3):
                    pass_on(chunk, slot, j, 0, plus)
                pass_on(chunk, slot, j, 2, sibling)

        if slot == 0:
            pl.when(jnp.logical_not(root))(take)
        else:
            take()

    def fill_coulomb(k, carry):
        row = lax.broadcasted_iota(jnp.int32, (N, N), 0)
        column = lax.broadcasted_iota(jnp.int32, (N, N), 1)
        middle = jnp.full((N, N), me * SLAB + k, jnp.int32)
        total = signed_square(row) + signed_square(middle) + signed_square(column)
        scale = CELL * CELL / np.pi / float(N) ** 3
        coulomb[k] = jnp.where(total > 0, scale / jnp.maximum(total, 1.0), 0.0)
        return carry

    lax.fori_loop(0, SLAB, fill_coulomb, 0)
    for load in loads[1:]:
        load.wait()

    def forward(p, j):
        r_a, r_b = round_of(2 * p), round_of(2 * p + 1)
        rows = []
        for i in range(2):
            o = orb[2 * j + i]
            rows.append(jnp.concatenate([o * srcs[r_a, 2 * j + i], o * srcs[r_b, 2 * j + i]], axis=1))
        along_z = from_right(jnp.concatenate(rows, axis=0), rights[0])
        real = jnp.concatenate([along_z[:N, :N], along_z[N:, :N]], axis=1)
        imag = jnp.concatenate([along_z[:N, N:], along_z[N:, N:]], axis=1)
        along_y = from_left(lefts[0], jnp.concatenate([real, imag], axis=0))
        for i in range(2):
            for part in range(2):
                send_a[p, 2 * j + i, part] = along_y[part * N : (part + 1) * N, i * N : (i + 1) * N]
        place = pl.ds(me * SLAB + 2 * j, 2)

        def block(f):
            return send_a.at[p, planes(j), :, pl.ds(pl.multiple_of(f * SLAB, SLAB), SLAB), :]

        for step in (5, 7, 6, 1, 3, 2, 4):
            f = peer_index(step)
            remote(
                block(f), recv_b.at[p, place], a_send.at[p], a_recv.at[p], {"band": band, "fft": f}
            ).start()
        pltpu.make_async_copy(block(me), recv_b.at[p, place], a_recv.at[p]).start()

    behind = {0: 0, 1: jnp.where(even, LAG, 1), 3: jnp.where(even, 6, 9), 2: jnp.where(even, 11, 9)}

    def relay(i):
        for slot in (0, 1, 3, 2):
            j = i - behind[slot]

            @pl.when(jnp.logical_and(j >= 0, j < STEPS))
            def _():
                arrive(slot, j)

    def first_steps(i, carry):
        relay(i)

        @pl.when(i >= LAG)
        def _():
            forward(0, i - LAG)

        return carry

    def second_steps(i, carry):
        relay(i)
        forward(1, i - STEPS - LAG)
        return carry

    def middle(p):
        pltpu.make_async_copy(recv_b.at[p], recv_b.at[p], a_recv.at[p]).wait()
        flat_in = recv_b.at[p].reshape(N * 2 * SLAB, N)
        flat_out = back.at[p].reshape(N * 2 * SLAB, N)

        def rows(part, k):
            return pl.ds(part * SLAB + k, N, stride=2 * SLAB)

        def body(i, carry):
            blocks = [
                jnp.concatenate([flat_in[rows(part, 2 * i), :], flat_in[rows(part, 2 * i + 1), :]], axis=1)
                for part in range(2)
            ]
            spectrum = from_left(lefts[0], jnp.concatenate(blocks, axis=0))
            weight = jnp.concatenate([coulomb[2 * i], coulomb[2 * i + 1]], axis=1)
            spectrum = spectrum * jnp.concatenate([weight, weight], axis=0)
            result = from_left(lefts[1], spectrum)
            for part in range(2):
                for n in range(2):
                    flat_out[rows(part, 2 * i + n), :] = result[part * N : (part + 1) * N, n * N : (n + 1) * N]
            return carry

        lax.fori_loop(0, SLAB // 2, body, 0)

    def give(p, j, carry):
        def place(ref):
            return ref.at[p, planes(j), :, pl.ds(pl.multiple_of(me * SLAB, SLAB), SLAB), :]

        for step in (5, 7, 6, 1, 3, 2, 4):
            f = peer_index(step)
            remote(
                back.at[p, pl.ds(f * SLAB + 2 * j, 2)], place(recv_c), c_send.at[p], c_recv.at[p, j],
                {"band": band, "fft": f},
            ).start()
        pltpu.make_async_copy(
            back.at[p, pl.ds(me * SLAB + 2 * j, 2)], place(recv_c), c_recv.at[p, j]
        ).start()
        return carry

    def inverse(p, j):
        chunk = recv_c.at[p, planes(j)]
        pltpu.make_async_copy(chunk, chunk, c_recv.at[p, j]).wait()
        parts_in = [
            jnp.concatenate([recv_c[p, 2 * j, part], recv_c[p, 2 * j + 1, part]], axis=1) for part in range(2)
        ]
        along_y = from_left(lefts[1], jnp.concatenate(parts_in, axis=0))
        rows = [
            jnp.concatenate([along_y[:N, i * N : (i + 1) * N], along_y[N:, i * N : (i + 1) * N]], axis=1)
            for i in range(2)
        ]
        potential = from_right(jnp.concatenate(rows, axis=0), rights[1])
        r_a, r_b = round_of(2 * p), round_of(2 * p + 1)
        for i in range(2):
            pot_a = potential[i * N : (i + 1) * N, :N]
            pot_b = potential[i * N : (i + 1) * N, N:]
            share = srcs[r_a, 2 * j + i] * pot_a + srcs[r_b, 2 * j + i] * pot_b
            if p > 0:
                share = own[2 * j + i] + share
            own[2 * j + i] = share
            o = orb[2 * j + i]
            terms[p, j, i, 0] = o * pot_a
            terms[p, j, i, 1] = o * pot_b
        remote(
            terms.at[p, j, 1 - core], summed.at[p, j], t_send.at[p], t_recv.at[p, j], sibling
        ).start()

    def spread(p, j):
        chunk = summed.at[p, j]
        pltpu.make_async_copy(chunk, chunk, t_recv.at[p, j]).wait()
        summed[p, j] = summed[p, j] + terms[p, j, core]

        def rows(z_at):
            return summed.at[p, j, :, pl.ds(pl.multiple_of(z_at * 16, 16), 16), :]

        for step in (4, 3, 5, 2, 6, 1, 7):
            z_at = lax.rem(z + step, ZS)
            remote(
                rows(z_at), gathered.at[z, pl.ds(2 * p, 2), j], z_send.at[p], z_recv.at[j], device(z_at, x_hi, core)
            ).start()
        gathered[z, pl.ds(2 * p, 2), j] = summed[p, j, :, pl.ds(pl.multiple_of(z * 16, 16), 16), :]

    others = (
        (1 - x_hi, core, across), (x_hi, 1 - core, sibling), (1 - x_hi, 1 - core, device(z, 1 - x_hi, 1 - core)),
    )

    def last(j, n):
        x_hi_at, core_at, target = others[n]
        return remote(
            folded.at[j, x_hi_at, core_at], folded_in.at[n, j], x_send.at[n], x_recv.at[n, j], target
        )

    def fold(j):
        arrived = gathered.at[pl.ds(0, 7), :, j]
        pltpu.make_async_copy(arrived, arrived, z_recv.at[j]).wait()
        totals = []
        for r in range(ROUNDS):
            total = gathered[0, r, j]
            for z_at in range(1, ZS):
                total = total + gathered[z_at, (r - z_at // 2) % ROUNDS, j]
            totals.append(total)
        for x_hi_at in range(2):
            for core_at in range(2):
                for n in range(2):
                    rows = slice(8 * x_hi_at + 4 * core_at, 8 * x_hi_at + 4 * core_at + 4)
                    folded[j, x_hi_at, core_at, n] = jnp.concatenate(
                        [totals[2 * n][rows], totals[2 * n + 1][rows]], axis=0
                    )
        for n in range(3):
            last(j, n).start()

    def write(j):
        for n in range(3):
            last(j, n).wait_recv()
        mine = folded[j, x_hi, core] + folded_in[0, j]
        theirs = folded_in[1, j] + folded_in[2, j]
        for r in range(ROUNDS):
            rows = slice(4 * (r % 2), 4 * (r % 2) + 4)
            out[r, 2 * j + core] = mine[r // 2, rows]
            out[r, 2 * j + 1 - core] = theirs[r // 2, rows]

    def second_half(p, stages, i, carry):
        for late, stage in stages:
            j = i - late

            @pl.when(jnp.logical_and(j >= 0, j < STEPS))
            def _():
                stage(j)

        return carry

    stages = [[(0, functools.partial(inverse, p)), (1, functools.partial(spread, p))] for p in range(PACKS)]
    stages[1] += [(3, fold), (5, write)]

    def finish(p, start, stop):
        lax.fori_loop(start, stop, functools.partial(second_half, p, stages[p]), 0)

    lax.fori_loop(0, STEPS + LAG, first_steps, 0)
    lax.fori_loop(STEPS + LAG, STEPS + LAG + AHEAD, second_steps, 0)
    middle(0)
    lax.fori_loop(0, STEPS - AHEAD, functools.partial(give, 0), 0)
    lax.fori_loop(STEPS + LAG + AHEAD, 2 * STEPS + LAG, second_steps, 0)
    lax.fori_loop(STEPS - AHEAD, STEPS, functools.partial(give, 0), 0)
    finish(0, 0, STEPS - AHEAD)
    middle(1)
    lax.fori_loop(0, STEPS, functools.partial(give, 1), 0)
    finish(0, STEPS - AHEAD, STEPS + 1)
    finish(1, 0, STEPS + 5)

    def sent(ref, sem):
        pltpu.make_async_copy(ref, ref, sem).wait()

    for p in range(PACKS):
        sent(send_a.at[p, pl.ds(0, 14)], a_send.at[p])
        sent(back.at[p, pl.ds(0, 112)], c_send.at[p])
        sent(summed.at[p], t_send.at[p])
        sent(summed.at[p, pl.ds(0, 7)], z_send.at[p])
    for n in range(3):
        sent(folded_in.at[n], x_send.at[n])

    @pl.when(lead)
    def _():
        for slot, kind in ((0, 0), (0, 2), (1, 2), (2, 2), (3, 0), (3, 2)):
            sent(srcs.at[slot], src_send.at[slot, kind])

        @pl.when(even)
        def _():
            sent(srcs.at[0], src_send.at[0, 1])
            sent(srcs.at[1], src_send.at[1, 1])
            sent(srcs.at[0, pl.ds(0, 2 * EARLY)], src_send.at[0, 4])

        @pl.when(jnp.logical_not(even))
        def _():
            sent(srcs.at[1, pl.ds(2 * EARLY, SLAB - 2 * EARLY)], src_send.at[1, 1])

        @pl.when(root)
        def _():
            sent(srcs.at[0], src_send.at[0, 3])


def local(rights, lefts, orbitals):
    f32 = jnp.float32
    dma = pltpu.SemaphoreType.DMA
    vmem = pl.BlockSpec(memory_space=pltpu.VMEM)
    own, source = pl.pallas_call(
        kernel,
        out_shape=(
            jax.ShapeDtypeStruct((SLAB, N, N), f32),
            jax.ShapeDtypeStruct((ROUNDS, SLAB, 4, N), f32),
        ),
        in_specs=[pl.BlockSpec(memory_space=pltpu.HBM)] * 3,
        out_specs=(vmem, vmem),
        scratch_shapes=[
            pltpu.VMEM((SLAB, N, N), f32),
            pltpu.VMEM(rights.shape, rights.dtype),
            pltpu.VMEM(lefts.shape, lefts.dtype),
            pltpu.VMEM((ROUNDS, SLAB, N, N), f32),
            pltpu.VMEM((PACKS, SLAB, 2, N, N), f32),
            pltpu.VMEM((PACKS, N, 2, SLAB, N), f32),
            pltpu.VMEM((PACKS, N, 2, SLAB, N), f32),
            pltpu.VMEM((PACKS, SLAB, 2, N, N), f32),
            pltpu.VMEM((PACKS, STEPS, 2, 2, N, N), f32),
            pltpu.VMEM((PACKS, STEPS, 2, N, N), f32),
            pltpu.VMEM((ZS, ROUNDS, STEPS, 16, N), f32),
            pltpu.VMEM((SLAB, N, N), f32),
            pltpu.VMEM((STEPS, 2, 2, 2, 8, N), f32),
            pltpu.VMEM((3, STEPS, 2, 8, N), f32),
            dma((3,)),
            dma((ROUNDS, STEPS)),
            dma((ROUNDS, 5)),
            dma((PACKS,)),
            dma((PACKS,)),
            dma((PACKS, STEPS)),
            dma((PACKS,)),
            dma((PACKS, STEPS)),
            dma((PACKS,)),
            dma((STEPS,)),
            dma((PACKS,)),
            dma((3, STEPS)),
            dma((3,)),
        ],
        compiler_params=pltpu.CompilerParams(
            collective_id=0, has_side_effects=True, vmem_limit_bytes=56 * 2**20
        ),
        name="exchange",
    )(orbitals[0], rights, lefts)
    return own[None], source


def solution(mesh):
    tables = [jnp.asarray(table) for table in matrices()]
    in_specs = (P("band", "fft", None, None),)
    out_specs = (P("band", "fft", None, None), P(None, "fft", "band", None))
    body = functools.partial(local, *tables)
    return jax.shard_map(body, mesh=mesh, in_specs=in_specs, out_specs=out_specs, check_vma=False)
```

```python
import functools

import jax
import jax.numpy as jnp
import ml_dtypes
import numpy as np
from jax import lax
from jax.experimental import pallas as pl
from jax.experimental.pallas import tpu as pltpu
from jax.sharding import PartitionSpec as P

N = 128
ROUNDS = 4
SLAB = 16
STEPS = 8
PACKS = 2
ZS = 8
CELL = 51.3
LAG = 3
EARLY = 4
MESH = pl.DeviceIdType.MESH


def matrices():
    index = np.arange(N)
    angle = 2.0 * np.pi * (np.outer(index, index) % N) / N
    cosine, sine = np.cos(angle), np.sin(angle)
    forward = np.block([[cosine, -sine], [sine, cosine]])

    def split(matrix):
        high = matrix.astype(np.float32).astype(ml_dtypes.bfloat16)
        low = (matrix - high.astype(np.float64)).astype(np.float32).astype(ml_dtypes.bfloat16)
        return high, low

    def right(matrix):
        high, low = split(matrix)
        return np.concatenate([high, high, low], axis=0)

    def left(matrix):
        high, low = split(matrix)
        return np.concatenate([high, high, low], axis=1)

    return np.stack([right(forward), right(forward.T)]), np.stack([left(forward.T), left(forward)])


def parts(value, axis):
    high = value.astype(jnp.bfloat16)
    low = (value - high.astype(jnp.float32)).astype(jnp.bfloat16)
    return jnp.concatenate([high, low, high], axis=axis)


def from_right(value, matrix):
    return jnp.dot(parts(value, 1), matrix, preferred_element_type=jnp.float32)


def from_left(matrix, value):
    return jnp.dot(matrix, parts(value, 0), preferred_element_type=jnp.float32)


def signed_square(index):
    signed = jnp.where(index <= N // 2, index, index - N)
    return (signed * signed).astype(jnp.float32)


def kernel(
    orb_in, rights_in, lefts_in, own, out,
    orb, rights, lefts, srcs, send_a, recv_b, back, recv_c, terms, summed, gathered, coulomb, folded, folded_in,
    in_sem, src_recv, src_send, a_recv, a_send, c_recv, c_send, t_recv, t_send, z_recv, z_send, x_recv, x_send,
):
    band = lax.axis_index("band")
    me = lax.axis_index("fft")
    z = band // 4
    x_hi = lax.rem(band // 2, 2)
    core = lax.rem(band, 2)
    x_lo = me // 4
    y = lax.rem(me, 4)
    even = lax.rem(z, 2) == 0
    root = jnp.logical_and(jnp.logical_and(even, x_hi == 0), core == 0)
    lead = core == 0

    loads = [
        pltpu.make_async_copy(src, dst, in_sem.at[i])
        for i, (src, dst) in enumerate(((orb_in, orb), (rights_in, rights), (lefts_in, lefts)))
    ]
    for load in loads:
        load.start()

    def device(z_at, x_hi_at, core_at):
        return {"band": z_at * 4 + x_hi_at * 2 + core_at, "fft": me}

    plus = device(lax.rem(z + 1, ZS), x_hi, core)
    minus = device(lax.rem(z + ZS - 1, ZS), x_hi, core)
    minus2 = device(lax.rem(z + ZS - 2, ZS), x_hi, core)
    sibling = device(z, x_hi, 1 - core)
    across = device(z, 1 - x_hi, core)

    def peer_index(step):
        d_lo, d_y = step // 4, lax.rem(step, 4)
        return lax.rem(x_lo + d_lo, 2) * 4 + lax.rem(y + d_y, 4)

    barrier = pltpu.get_barrier_semaphore()

    def signal(target):
        pl.semaphore_signal(barrier, inc=1, device_id=target, device_id_type=MESH)

    for step in range(1, 8):
        signal({"band": band, "fft": peer_index(step)})
    for step in range(1, ZS):
        signal(device(lax.rem(z + step, ZS), x_hi, core))
    signal(sibling)
    signal(across)
    signal(device(z, 1 - x_hi, 1 - core))
    loads[0].wait()
    pl.semaphore_wait(barrier, 17)

    def round_of(slot):
        return lax.rem(z // 2 + slot, ROUNDS)

    def planes(j):
        return pl.ds(2 * j, 2)

    def remote(src, dst, send_sem, recv_sem, target):
        return pltpu.make_async_remote_copy(
            src_ref=src, dst_ref=dst, send_sem=send_sem, recv_sem=recv_sem, device_id=target, device_id_type=MESH
        )

    def pass_on(src, slot, j, kind, target):
        r = round_of(slot)
        remote(src, srcs.at[r, planes(j)], src_send.at[slot, kind], src_recv.at[r, j], target).start()

    def pass_early(chunk, j):
        @pl.when(j < EARLY)
        def _():
            pass_on(chunk, 0, j, 4, minus2)

    def pass_own(j):
        chunk = orb.at[planes(j)]
        pass_on(chunk, 0, j, 3, across)
        pass_early(chunk, j)
        pass_on(chunk, 0, j, 1, minus)
        pass_on(chunk, 0, j, 0, plus)
        pass_on(chunk, 0, j, 2, sibling)

    @pl.when(root)
    def _():
        for j in range(LAG):
            pass_own(j)

        def fill(j, carry):
            srcs[round_of(0), planes(j)] = orb[planes(j)]
            return carry

        lax.fori_loop(0, STEPS, fill, 0)

    def arrive(slot, j):
        r = round_of(slot)
        chunk = srcs.at[r, planes(j)]

        def take():
            pltpu.make_async_copy(chunk, chunk, src_recv.at[r, j]).wait()

            @pl.when(lead)
            def _():
                if slot == 1:

                    @pl.when(jnp.logical_or(even, j >= EARLY))
                    def _():
                        pass_on(chunk, slot, j, 1, minus)

                if slot == 0:

                    @pl.when(even)
                    def _():
                        pass_early(chunk, j)
                        pass_on(chunk, slot, j, 1, minus)

                if slot in (0, 3):
                    pass_on(chunk, slot, j, 0, plus)
                pass_on(chunk, slot, j, 2, sibling)

        if slot == 0:
            pl.when(jnp.logical_not(root))(take)
        else:
            take()

    def fill_coulomb(k, carry):
        row = lax.broadcasted_iota(jnp.int32, (N, N), 0)
        column = lax.broadcasted_iota(jnp.int32, (N, N), 1)
        middle = jnp.full((N, N), me * SLAB + k, jnp.int32)
        total = signed_square(row) + signed_square(middle) + signed_square(column)
        scale = CELL * CELL / np.pi / float(N) ** 3
        coulomb[k] = jnp.where(total > 0, scale / jnp.maximum(total, 1.0), 0.0)
        return carry

    lax.fori_loop(0, SLAB, fill_coulomb, 0)
    for load in loads[1:]:
        load.wait()

    def forward(p, j):
        r_a, r_b = round_of(2 * p), round_of(2 * p + 1)
        rows = []
        for i in range(2):
            o = orb[2 * j + i]
            rows.append(jnp.concatenate([o * srcs[r_a, 2 * j + i], o * srcs[r_b, 2 * j + i]], axis=1))
        along_z = from_right(jnp.concatenate(rows, axis=0), rights[0])
        real = jnp.concatenate([along_z[:N, :N], along_z[N:, :N]], axis=1)
        imag = jnp.concatenate([along_z[:N, N:], along_z[N:, N:]], axis=1)
        along_y = from_left(lefts[0], jnp.concatenate([real, imag], axis=0))
        for i in range(2):
            for part in range(2):
                send_a[p, 2 * j + i, part] = along_y[part * N : (part + 1) * N, i * N : (i + 1) * N]
        place = pl.ds(me * SLAB + 2 * j, 2)

        def block(f):
            return send_a.at[p, planes(j), :, pl.ds(pl.multiple_of(f * SLAB, SLAB), SLAB), :]

        for step in (5, 7, 6, 1, 3, 2, 4):
            f = peer_index(step)
            remote(
                block(f), recv_b.at[p, place], a_send.at[p], a_recv.at[p], {"band": band, "fft": f}
            ).start()
        pltpu.make_async_copy(block(me), recv_b.at[p, place], a_recv.at[p]).start()

    behind = {0: 0, 1: jnp.where(even, LAG, 1), 3: jnp.where(even, 6, 9), 2: jnp.where(even, 11, 9)}

    def relay(i):
        for slot in (0, 1, 3, 2):
            j = i - behind[slot]

            @pl.when(jnp.logical_and(j >= 0, j < STEPS))
            def _():
                arrive(slot, j)

    def first_steps(i, carry):
        @pl.when(jnp.logical_and(root, jnp.logical_and(i >= LAG, i < STEPS)))
        def _():
            pass_own(i)

        relay(i)

        @pl.when(i >= LAG)
        def _():
            forward(0, i - LAG)

        return carry

    def second_steps(i, carry):
        relay(i)
        forward(1, i - STEPS - LAG)
        return carry

    lax.fori_loop(0, STEPS + LAG, first_steps, 0)
    lax.fori_loop(STEPS + LAG, 2 * STEPS + LAG, second_steps, 0)

    def middle(p):
        pltpu.make_async_copy(recv_b.at[p], recv_b.at[p], a_recv.at[p]).wait()
        flat_in = recv_b.at[p].reshape(N * 2 * SLAB, N)
        flat_out = back.at[p].reshape(N * 2 * SLAB, N)

        def rows(part, k):
            return pl.ds(part * SLAB + k, N, stride=2 * SLAB)

        def body(i, carry):
            blocks = [
                jnp.concatenate([flat_in[rows(part, 2 * i), :], flat_in[rows(part, 2 * i + 1), :]], axis=1)
                for part in range(2)
            ]
            spectrum = from_left(lefts[0], jnp.concatenate(blocks, axis=0))
            weight = jnp.concatenate([coulomb[2 * i], coulomb[2 * i + 1]], axis=1)
            spectrum = spectrum * jnp.concatenate([weight, weight], axis=0)
            result = from_left(lefts[1], spectrum)
            for part in range(2):
                for n in range(2):
                    flat_out[rows(part, 2 * i + n), :] = result[part * N : (part + 1) * N, n * N : (n + 1) * N]
            return carry

        lax.fori_loop(0, SLAB // 2, body, 0)

        def give(j, carry):
            def place(ref):
                return ref.at[p, planes(j), :, pl.ds(pl.multiple_of(me * SLAB, SLAB), SLAB), :]

            for step in (5, 7, 6, 1, 3, 2, 4):
                f = peer_index(step)
                remote(
                    back.at[p, pl.ds(f * SLAB + 2 * j, 2)], place(recv_c), c_send.at[p], c_recv.at[p, j],
                    {"band": band, "fft": f},
                ).start()
            pltpu.make_async_copy(
                back.at[p, pl.ds(me * SLAB + 2 * j, 2)], place(recv_c), c_recv.at[p, j]
            ).start()
            return carry

        lax.fori_loop(0, STEPS, give, 0)

    for p in range(PACKS):
        middle(p)

    def inverse(p, j):
        chunk = recv_c.at[p, planes(j)]
        pltpu.make_async_copy(chunk, chunk, c_recv.at[p, j]).wait()
        parts_in = [
            jnp.concatenate([recv_c[p, 2 * j, part], recv_c[p, 2 * j + 1, part]], axis=1) for part in range(2)
        ]
        along_y = from_left(lefts[1], jnp.concatenate(parts_in, axis=0))
        rows = [
            jnp.concatenate([along_y[:N, i * N : (i + 1) * N], along_y[N:, i * N : (i + 1) * N]], axis=1)
            for i in range(2)
        ]
        potential = from_right(jnp.concatenate(rows, axis=0), rights[1])
        r_a, r_b = round_of(2 * p), round_of(2 * p + 1)
        for i in range(2):
            pot_a = potential[i * N : (i + 1) * N, :N]
            pot_b = potential[i * N : (i + 1) * N, N:]
            share = srcs[r_a, 2 * j + i] * pot_a + srcs[r_b, 2 * j + i] * pot_b
            if p > 0:
                share = own[2 * j + i] + share
            own[2 * j + i] = share
            o = orb[2 * j + i]
            terms[p, j, i, 0] = o * pot_a
            terms[p, j, i, 1] = o * pot_b
        remote(
            terms.at[p, j, 1 - core], summed.at[p, j], t_send.at[p], t_recv.at[p, j], sibling
        ).start()

    def spread(p, j):
        chunk = summed.at[p, j]
        pltpu.make_async_copy(chunk, chunk, t_recv.at[p, j]).wait()
        summed[p, j] = summed[p, j] + terms[p, j, core]

        def rows(z_at):
            return summed.at[p, j, :, pl.ds(pl.multiple_of(z_at * 16, 16), 16), :]

        for step in (4, 3, 5, 2, 6, 1, 7):
            z_at = lax.rem(z + step, ZS)
            remote(
                rows(z_at), gathered.at[z, pl.ds(2 * p, 2), j], z_send.at[p], z_recv.at[j], device(z_at, x_hi, core)
            ).start()
        gathered[z, pl.ds(2 * p, 2), j] = summed[p, j, :, pl.ds(pl.multiple_of(z * 16, 16), 16), :]

    others = (
        (1 - x_hi, core, across), (x_hi, 1 - core, sibling), (1 - x_hi, 1 - core, device(z, 1 - x_hi, 1 - core)),
    )

    def last(j, n):
        x_hi_at, core_at, target = others[n]
        return remote(
            folded.at[j, x_hi_at, core_at], folded_in.at[n, j], x_send.at[n], x_recv.at[n, j], target
        )

    def fold(j):
        arrived = gathered.at[pl.ds(0, 7), :, j]
        pltpu.make_async_copy(arrived, arrived, z_recv.at[j]).wait()
        totals = []
        for r in range(ROUNDS):
            total = gathered[0, r, j]
            for z_at in range(1, ZS):
                total = total + gathered[z_at, (r - z_at // 2) % ROUNDS, j]
            totals.append(total)
        for x_hi_at in range(2):
            for core_at in range(2):
                for n in range(2):
                    rows = slice(8 * x_hi_at + 4 * core_at, 8 * x_hi_at + 4 * core_at + 4)
                    folded[j, x_hi_at, core_at, n] = jnp.concatenate(
                        [totals[2 * n][rows], totals[2 * n + 1][rows]], axis=0
                    )
        for n in range(3):
            last(j, n).start()

    def write(j):
        for n in range(3):
            last(j, n).wait_recv()
        mine = folded[j, x_hi, core] + folded_in[0, j]
        theirs = folded_in[1, j] + folded_in[2, j]
        for r in range(ROUNDS):
            rows = slice(4 * (r % 2), 4 * (r % 2) + 4)
            out[r, 2 * j + core] = mine[r // 2, rows]
            out[r, 2 * j + 1 - core] = theirs[r // 2, rows]

    def second_half(p, stages, i, carry):
        for late, stage in stages:
            j = i - late

            @pl.when(jnp.logical_and(j >= 0, j < STEPS))
            def _():
                stage(j)

        return carry

    for p in range(PACKS):
        stages = [(0, functools.partial(inverse, p)), (1, functools.partial(spread, p))]
        if p == PACKS - 1:
            stages += [(3, fold), (5, write)]
        lax.fori_loop(0, STEPS + stages[-1][0], functools.partial(second_half, p, stages), 0)

    def sent(ref, sem):
        pltpu.make_async_copy(ref, ref, sem).wait()

    for p in range(PACKS):
        sent(send_a.at[p, pl.ds(0, 14)], a_send.at[p])
        sent(back.at[p, pl.ds(0, 112)], c_send.at[p])
        sent(summed.at[p], t_send.at[p])
        sent(summed.at[p, pl.ds(0, 7)], z_send.at[p])
    for n in range(3):
        sent(folded_in.at[n], x_send.at[n])

    @pl.when(lead)
    def _():
        for slot, kind in ((0, 0), (0, 2), (1, 2), (2, 2), (3, 0), (3, 2)):
            sent(srcs.at[slot], src_send.at[slot, kind])

        @pl.when(even)
        def _():
            sent(srcs.at[0], src_send.at[0, 1])
            sent(srcs.at[1], src_send.at[1, 1])
            sent(srcs.at[0, pl.ds(0, 2 * EARLY)], src_send.at[0, 4])

        @pl.when(jnp.logical_not(even))
        def _():
            sent(srcs.at[1, pl.ds(2 * EARLY, SLAB - 2 * EARLY)], src_send.at[1, 1])

        @pl.when(root)
        def _():
            sent(srcs.at[0], src_send.at[0, 3])


def local(rights, lefts, orbitals):
    f32 = jnp.float32
    dma = pltpu.SemaphoreType.DMA
    vmem = pl.BlockSpec(memory_space=pltpu.VMEM)
    own, source = pl.pallas_call(
        kernel,
        out_shape=(
            jax.ShapeDtypeStruct((SLAB, N, N), f32),
            jax.ShapeDtypeStruct((ROUNDS, SLAB, 4, N), f32),
        ),
        in_specs=[pl.BlockSpec(memory_space=pltpu.HBM)] * 3,
        out_specs=(vmem, vmem),
        scratch_shapes=[
            pltpu.VMEM((SLAB, N, N), f32),
            pltpu.VMEM(rights.shape, rights.dtype),
            pltpu.VMEM(lefts.shape, lefts.dtype),
            pltpu.VMEM((ROUNDS, SLAB, N, N), f32),
            pltpu.VMEM((PACKS, SLAB, 2, N, N), f32),
            pltpu.VMEM((PACKS, N, 2, SLAB, N), f32),
            pltpu.VMEM((PACKS, N, 2, SLAB, N), f32),
            pltpu.VMEM((PACKS, SLAB, 2, N, N), f32),
            pltpu.VMEM((PACKS, STEPS, 2, 2, N, N), f32),
            pltpu.VMEM((PACKS, STEPS, 2, N, N), f32),
            pltpu.VMEM((ZS, ROUNDS, STEPS, 16, N), f32),
            pltpu.VMEM((SLAB, N, N), f32),
            pltpu.VMEM((STEPS, 2, 2, 2, 8, N), f32),
            pltpu.VMEM((3, STEPS, 2, 8, N), f32),
            dma((3,)),
            dma((ROUNDS, STEPS)),
            dma((ROUNDS, 5)),
            dma((PACKS,)),
            dma((PACKS,)),
            dma((PACKS, STEPS)),
            dma((PACKS,)),
            dma((PACKS, STEPS)),
            dma((PACKS,)),
            dma((STEPS,)),
            dma((PACKS,)),
            dma((3, STEPS)),
            dma((3,)),
        ],
        compiler_params=pltpu.CompilerParams(
            collective_id=0, has_side_effects=True, vmem_limit_bytes=56 * 2**20
        ),
        name="exchange",
    )(orbitals[0], rights, lefts)
    return own[None], source


def solution(mesh):
    tables = [jnp.asarray(table) for table in matrices()]
    in_specs = (P("band", "fft", None, None),)
    out_specs = (P("band", "fft", None, None), P(None, "fft", "band", None))
    body = functools.partial(local, *tables)
    return jax.shard_map(body, mesh=mesh, in_specs=in_specs, out_specs=out_specs, check_vma=False)
```

```python
import functools

import jax
import jax.numpy as jnp
import ml_dtypes
import numpy as np
from jax import lax
from jax.experimental import pallas as pl
from jax.experimental.pallas import tpu as pltpu
from jax.sharding import PartitionSpec as P

N = 128
ROUNDS = 4
SLAB = 16
STEPS = 8
DEPTH = 2
PACKS = 2
ZS = 8
CELL = 51.3
LAG = 3
EARLY = 4
MESH = pl.DeviceIdType.MESH


def matrices():
    index = np.arange(N)
    angle = 2.0 * np.pi * (np.outer(index, index) % N) / N
    cosine, sine = np.cos(angle), np.sin(angle)
    forward = np.block([[cosine, -sine], [sine, cosine]])

    def split(matrix):
        high = matrix.astype(np.float32).astype(ml_dtypes.bfloat16)
        low = (matrix - high.astype(np.float64)).astype(np.float32).astype(ml_dtypes.bfloat16)
        return high, low

    def right(matrix):
        high, low = split(matrix)
        return np.concatenate([high, high, low], axis=0)

    def left(matrix):
        high, low = split(matrix)
        return np.concatenate([high, high, low], axis=1)

    return np.stack([right(forward), right(forward.T)]), np.stack([left(forward.T), left(forward)])


def parts(value, axis):
    high = value.astype(jnp.bfloat16)
    low = (value - high.astype(jnp.float32)).astype(jnp.bfloat16)
    return jnp.concatenate([high, low, high], axis=axis)


def from_right(value, matrix):
    return jnp.dot(parts(value, 1), matrix, preferred_element_type=jnp.float32)


def from_left(matrix, value):
    return jnp.dot(matrix, parts(value, 0), preferred_element_type=jnp.float32)


def signed_square(index):
    signed = jnp.where(index <= N // 2, index, index - N)
    return (signed * signed).astype(jnp.float32)


def kernel(
    orb_in, rights_in, lefts_in, own, out,
    orb, rights, lefts, srcs, send_a, recv_b, back, recv_c, terms, summed, gathered, coulomb, folded, folded_in,
    in_sem, src_recv, src_send, a_recv, a_send, c_recv, c_send, t_recv, t_send, z_recv, z_send, x_recv, x_send,
):
    band = lax.axis_index("band")
    me = lax.axis_index("fft")
    z = band // 4
    x_hi = lax.rem(band // 2, 2)
    core = lax.rem(band, 2)
    x_lo = me // 4
    y = lax.rem(me, 4)
    even = lax.rem(z, 2) == 0
    root = jnp.logical_and(jnp.logical_and(even, x_hi == 0), core == 0)
    lead = core == 0

    loads = [
        pltpu.make_async_copy(src, dst, in_sem.at[i])
        for i, (src, dst) in enumerate(((orb_in, orb), (rights_in, rights), (lefts_in, lefts)))
    ]
    for load in loads:
        load.start()

    def device(z_at, x_hi_at, core_at):
        return {"band": z_at * 4 + x_hi_at * 2 + core_at, "fft": me}

    plus = device(lax.rem(z + 1, ZS), x_hi, core)
    minus = device(lax.rem(z + ZS - 1, ZS), x_hi, core)
    minus2 = device(lax.rem(z + ZS - 2, ZS), x_hi, core)
    sibling = device(z, x_hi, 1 - core)
    across = device(z, 1 - x_hi, core)

    def peer_index(step):
        d_lo, d_y = step // 4, lax.rem(step, 4)
        return lax.rem(x_lo + d_lo, 2) * 4 + lax.rem(y + d_y, 4)

    barrier = pltpu.get_barrier_semaphore()

    def signal(target):
        pl.semaphore_signal(barrier, inc=1, device_id=target, device_id_type=MESH)

    for step in range(1, 8):
        signal({"band": band, "fft": peer_index(step)})
    for step in range(1, ZS):
        signal(device(lax.rem(z + step, ZS), x_hi, core))
    signal(sibling)
    signal(across)
    signal(device(z, 1 - x_hi, 1 - core))
    loads[0].wait()
    pl.semaphore_wait(barrier, 17)

    def round_of(slot):
        return lax.rem(z // 2 + slot, ROUNDS)

    def planes(j):
        return pl.ds(2 * j, 2)

    def remote(src, dst, send_sem, recv_sem, target):
        return pltpu.make_async_remote_copy(
            src_ref=src, dst_ref=dst, send_sem=send_sem, recv_sem=recv_sem, device_id=target, device_id_type=MESH
        )

    def pass_on(src, slot, j, kind, target):
        r = round_of(slot)
        remote(src, srcs.at[r, planes(j)], src_send.at[slot, kind], src_recv.at[r, j], target).start()

    def pass_early(chunk, j):
        @pl.when(j < EARLY)
        def _():
            pass_on(chunk, 0, j, 4, minus2)

    @pl.when(root)
    def _():
        def body(j, carry):
            chunk = orb.at[planes(j)]
            pass_on(chunk, 0, j, 3, across)
            pass_early(chunk, j)
            pass_on(chunk, 0, j, 1, minus)
            pass_on(chunk, 0, j, 0, plus)
            pass_on(chunk, 0, j, 2, sibling)
            return carry

        lax.fori_loop(0, STEPS, body, 0)

        def fill(j, carry):
            srcs[round_of(0), planes(j)] = orb[planes(j)]
            return carry

        lax.fori_loop(0, STEPS, fill, 0)

    def arrive(slot, j):
        r = round_of(slot)
        chunk = srcs.at[r, planes(j)]

        def take():
            pltpu.make_async_copy(chunk, chunk, src_recv.at[r, j]).wait()

            @pl.when(lead)
            def _():
                if slot == 1:

                    @pl.when(jnp.logical_or(even, j >= EARLY))
                    def _():
                        pass_on(chunk, slot, j, 1, minus)

                if slot == 0:

                    @pl.when(even)
                    def _():
                        pass_early(chunk, j)
                        pass_on(chunk, slot, j, 1, minus)

                if slot in (0, 3):
                    pass_on(chunk, slot, j, 0, plus)
                pass_on(chunk, slot, j, 2, sibling)

        if slot == 0:
            pl.when(jnp.logical_not(root))(take)
        else:
            take()

    def fill_coulomb(k, carry):
        row = lax.broadcasted_iota(jnp.int32, (N, N), 0)
        column = lax.broadcasted_iota(jnp.int32, (N, N), 1)
        middle = jnp.full((N, N), me * SLAB + k, jnp.int32)
        total = signed_square(row) + signed_square(middle) + signed_square(column)
        scale = CELL * CELL / np.pi / float(N) ** 3
        coulomb[k] = jnp.where(total > 0, scale / jnp.maximum(total, 1.0), 0.0)
        return carry

    lax.fori_loop(0, SLAB, fill_coulomb, 0)
    for load in loads[1:]:
        load.wait()

    def left_fwd(p, j):
        blocks = send_a.at[p, pl.ds(0, 2), :, pl.ds(0, 7 * SLAB), :]
        pltpu.make_async_copy(blocks, blocks, a_send.at[p, j]).wait()

    def forward(p, j):
        r_a, r_b = round_of(2 * p), round_of(2 * p + 1)
        rows = []
        for i in range(2):
            o = orb[2 * j + i]
            rows.append(jnp.concatenate([o * srcs[r_a, 2 * j + i], o * srcs[r_b, 2 * j + i]], axis=1))
        along_z = from_right(jnp.concatenate(rows, axis=0), rights[0])
        real = jnp.concatenate([along_z[:N, :N], along_z[N:, :N]], axis=1)
        imag = jnp.concatenate([along_z[:N, N:], along_z[N:, N:]], axis=1)
        along_y = from_left(lefts[0], jnp.concatenate([real, imag], axis=0))
        for i in range(2):
            for part in range(2):
                send_a[p, 2 * j + i, part] = along_y[part * N : (part + 1) * N, i * N : (i + 1) * N]
        place = pl.ds(me * SLAB + 2 * j, 2)

        def block(f):
            return send_a.at[p, planes(j), :, pl.ds(pl.multiple_of(f * SLAB, SLAB), SLAB), :]

        if p > 0:
            pl.when(j < DEPTH)(lambda: left_fwd(p - 1, j + STEPS - DEPTH))
        pl.when(j >= DEPTH)(lambda: left_fwd(p, j - DEPTH))

        for step in (5, 7, 6, 1, 3, 2, 4):
            f = peer_index(step)
            remote(
                block(f), recv_b.at[p, place], a_send.at[p, j], a_recv.at[p], {"band": band, "fft": f}
            ).start()
        pltpu.make_async_copy(block(me), recv_b.at[p, place], a_recv.at[p]).start()

    behind = {0: 0, 1: jnp.where(even, LAG, 1), 3: jnp.where(even, 6, 9), 2: jnp.where(even, 11, 9)}

    def relay(i):
        for slot in (0, 1, 3, 2):
            j = i - behind[slot]

            @pl.when(jnp.logical_and(j >= 0, j < STEPS))
            def _():
                arrive(slot, j)

    def first_steps(i, carry):
        relay(i)

        @pl.when(i >= LAG)
        def _():
            forward(0, i - LAG)

        return carry

    def second_steps(i, carry):
        relay(i)
        forward(1, i - STEPS - LAG)
        return carry

    lax.fori_loop(0, STEPS + LAG, first_steps, 0)
    lax.fori_loop(STEPS + LAG, 2 * STEPS + LAG, second_steps, 0)

    def middle(p):
        pltpu.make_async_copy(recv_b.at[p], recv_b.at[p], a_recv.at[p]).wait()
        flat_in = recv_b.at[p].reshape(N * 2 * SLAB, N)
        flat_out = back.at[p].reshape(N * 2 * SLAB, N)

        def rows(part, k):
            return pl.ds(part * SLAB + k, N, stride=2 * SLAB)

        def body(i, carry):
            blocks = [
                jnp.concatenate([flat_in[rows(part, 2 * i), :], flat_in[rows(part, 2 * i + 1), :]], axis=1)
                for part in range(2)
            ]
            spectrum = from_left(lefts[0], jnp.concatenate(blocks, axis=0))
            weight = jnp.concatenate([coulomb[2 * i], coulomb[2 * i + 1]], axis=1)
            spectrum = spectrum * jnp.concatenate([weight, weight], axis=0)
            result = from_left(lefts[1], spectrum)
            for part in range(2):
                for n in range(2):
                    flat_out[rows(part, 2 * i + n), :] = result[part * N : (part + 1) * N, n * N : (n + 1) * N]
            return carry

        lax.fori_loop(0, SLAB // 2, body, 0)

        def give(j, carry):
            def place(ref):
                return ref.at[p, planes(j), :, pl.ds(pl.multiple_of(me * SLAB, SLAB), SLAB), :]

            for step in (5, 7, 6, 1, 3, 2, 4):
                f = peer_index(step)
                remote(
                    back.at[p, pl.ds(f * SLAB + 2 * j, 2)], place(recv_c), c_send.at[p], c_recv.at[p, j],
                    {"band": band, "fft": f},
                ).start()
            pltpu.make_async_copy(
                back.at[p, pl.ds(me * SLAB + 2 * j, 2)], place(recv_c), c_recv.at[p, j]
            ).start()
            return carry

        lax.fori_loop(0, STEPS, give, 0)

    for p in range(PACKS):
        middle(p)

    def inverse(p, j):
        chunk = recv_c.at[p, planes(j)]
        pltpu.make_async_copy(chunk, chunk, c_recv.at[p, j]).wait()
        parts_in = [
            jnp.concatenate([recv_c[p, 2 * j, part], recv_c[p, 2 * j + 1, part]], axis=1) for part in range(2)
        ]
        along_y = from_left(lefts[1], jnp.concatenate(parts_in, axis=0))
        rows = [
            jnp.concatenate([along_y[:N, i * N : (i + 1) * N], along_y[N:, i * N : (i + 1) * N]], axis=1)
            for i in range(2)
        ]
        potential = from_right(jnp.concatenate(rows, axis=0), rights[1])
        r_a, r_b = round_of(2 * p), round_of(2 * p + 1)
        for i in range(2):
            pot_a = potential[i * N : (i + 1) * N, :N]
            pot_b = potential[i * N : (i + 1) * N, N:]
            share = srcs[r_a, 2 * j + i] * pot_a + srcs[r_b, 2 * j + i] * pot_b
            if p > 0:
                share = own[2 * j + i] + share
            own[2 * j + i] = share
            o = orb[2 * j + i]
            terms[p, j, i, 0] = o * pot_a
            terms[p, j, i, 1] = o * pot_b
        remote(
            terms.at[p, j, 1 - core], summed.at[p, j], t_send.at[p], t_recv.at[p, j], sibling
        ).start()

    def spread(p, j):
        chunk = summed.at[p, j]
        pltpu.make_async_copy(chunk, chunk, t_recv.at[p, j]).wait()
        summed[p, j] = summed[p, j] + terms[p, j, core]

        def rows(z_at):
            return summed.at[p, j, :, pl.ds(pl.multiple_of(z_at * 16, 16), 16), :]

        for step in (4, 3, 5, 2, 6, 1, 7):
            z_at = lax.rem(z + step, ZS)
            remote(
                rows(z_at), gathered.at[z, pl.ds(2 * p, 2), j], z_send.at[p], z_recv.at[j], device(z_at, x_hi, core)
            ).start()
        gathered[z, pl.ds(2 * p, 2), j] = summed[p, j, :, pl.ds(pl.multiple_of(z * 16, 16), 16), :]

    others = (
        (1 - x_hi, core, across), (x_hi, 1 - core, sibling), (1 - x_hi, 1 - core, device(z, 1 - x_hi, 1 - core)),
    )

    def last(j, n):
        x_hi_at, core_at, target = others[n]
        return remote(
            folded.at[j, x_hi_at, core_at], folded_in.at[n, j], x_send.at[n], x_recv.at[n, j], target
        )

    def fold(j):
        arrived = gathered.at[pl.ds(0, 7), :, j]
        pltpu.make_async_copy(arrived, arrived, z_recv.at[j]).wait()
        totals = []
        for r in range(ROUNDS):
            total = gathered[0, r, j]
            for z_at in range(1, ZS):
                total = total + gathered[z_at, (r - z_at // 2) % ROUNDS, j]
            totals.append(total)
        for x_hi_at in range(2):
            for core_at in range(2):
                for n in range(2):
                    rows = slice(8 * x_hi_at + 4 * core_at, 8 * x_hi_at + 4 * core_at + 4)
                    folded[j, x_hi_at, core_at, n] = jnp.concatenate(
                        [totals[2 * n][rows], totals[2 * n + 1][rows]], axis=0
                    )
        for n in range(3):
            last(j, n).start()

    def write(j):
        for n in range(3):
            last(j, n).wait_recv()
        mine = folded[j, x_hi, core] + folded_in[0, j]
        theirs = folded_in[1, j] + folded_in[2, j]
        for r in range(ROUNDS):
            rows = slice(4 * (r % 2), 4 * (r % 2) + 4)
            out[r, 2 * j + core] = mine[r // 2, rows]
            out[r, 2 * j + 1 - core] = theirs[r // 2, rows]

    def second_half(p, stages, i, carry):
        for late, stage in stages:
            j = i - late

            @pl.when(jnp.logical_and(j >= 0, j < STEPS))
            def _():
                stage(j)

        return carry

    for p in range(PACKS):
        stages = [(0, functools.partial(inverse, p)), (1, functools.partial(spread, p))]
        if p == PACKS - 1:
            stages += [(3, fold), (5, write)]
        lax.fori_loop(0, STEPS + stages[-1][0], functools.partial(second_half, p, stages), 0)

    for j in range(STEPS - DEPTH, STEPS):
        left_fwd(PACKS - 1, j)

    def sent(ref, sem):
        pltpu.make_async_copy(ref, ref, sem).wait()

    for p in range(PACKS):
        sent(back.at[p, pl.ds(0, 112)], c_send.at[p])
        sent(summed.at[p], t_send.at[p])
        sent(summed.at[p, pl.ds(0, 7)], z_send.at[p])
    for n in range(3):
        sent(folded_in.at[n], x_send.at[n])

    @pl.when(lead)
    def _():
        for slot, kind in ((0, 0), (0, 2), (1, 2), (2, 2), (3, 0), (3, 2)):
            sent(srcs.at[slot], src_send.at[slot, kind])

        @pl.when(even)
        def _():
            sent(srcs.at[0], src_send.at[0, 1])
            sent(srcs.at[1], src_send.at[1, 1])
            sent(srcs.at[0, pl.ds(0, 2 * EARLY)], src_send.at[0, 4])

        @pl.when(jnp.logical_not(even))
        def _():
            sent(srcs.at[1, pl.ds(2 * EARLY, SLAB - 2 * EARLY)], src_send.at[1, 1])

        @pl.when(root)
        def _():
            sent(srcs.at[0], src_send.at[0, 3])


def local(rights, lefts, orbitals):
    f32 = jnp.float32
    dma = pltpu.SemaphoreType.DMA
    vmem = pl.BlockSpec(memory_space=pltpu.VMEM)
    own, source = pl.pallas_call(
        kernel,
        out_shape=(
            jax.ShapeDtypeStruct((SLAB, N, N), f32),
            jax.ShapeDtypeStruct((ROUNDS, SLAB, 4, N), f32),
        ),
        in_specs=[pl.BlockSpec(memory_space=pltpu.HBM)] * 3,
        out_specs=(vmem, vmem),
        scratch_shapes=[
            pltpu.VMEM((SLAB, N, N), f32),
            pltpu.VMEM(rights.shape, rights.dtype),
            pltpu.VMEM(lefts.shape, lefts.dtype),
            pltpu.VMEM((ROUNDS, SLAB, N, N), f32),
            pltpu.VMEM((PACKS, SLAB, 2, N, N), f32),
            pltpu.VMEM((PACKS, N, 2, SLAB, N), f32),
            pltpu.VMEM((PACKS, N, 2, SLAB, N), f32),
            pltpu.VMEM((PACKS, SLAB, 2, N, N), f32),
            pltpu.VMEM((PACKS, STEPS, 2, 2, N, N), f32),
            pltpu.VMEM((PACKS, STEPS, 2, N, N), f32),
            pltpu.VMEM((ZS, ROUNDS, STEPS, 16, N), f32),
            pltpu.VMEM((SLAB, N, N), f32),
            pltpu.VMEM((STEPS, 2, 2, 2, 8, N), f32),
            pltpu.VMEM((3, STEPS, 2, 8, N), f32),
            dma((3,)),
            dma((ROUNDS, STEPS)),
            dma((ROUNDS, 5)),
            dma((PACKS,)),
            dma((PACKS, STEPS)),
            dma((PACKS, STEPS)),
            dma((PACKS,)),
            dma((PACKS, STEPS)),
            dma((PACKS,)),
            dma((STEPS,)),
            dma((PACKS,)),
            dma((3, STEPS)),
            dma((3,)),
        ],
        compiler_params=pltpu.CompilerParams(
            collective_id=0, has_side_effects=True, vmem_limit_bytes=56 * 2**20
        ),
        name="exchange",
    )(orbitals[0], rights, lefts)
    return own[None], source


def solution(mesh):
    tables = [jnp.asarray(table) for table in matrices()]
    in_specs = (P("band", "fft", None, None),)
    out_specs = (P("band", "fft", None, None), P(None, "fft", "band", None))
    body = functools.partial(local, *tables)
    return jax.shard_map(body, mesh=mesh, in_specs=in_specs, out_specs=out_specs, check_vma=False)
```

```python
import functools

import jax
import jax.numpy as jnp
import ml_dtypes
import numpy as np
from jax import lax
from jax.experimental import pallas as pl
from jax.experimental.pallas import tpu as pltpu
from jax.sharding import PartitionSpec as P

N = 128
ROUNDS = 4
SLAB = 16
STEPS = 8
DEPTH = 2
PACKS = 2
ZS = 8
CELL = 51.3
LAG = 3
EARLY = 4
MESH = pl.DeviceIdType.MESH


def matrices():
    index = np.arange(N)
    angle = 2.0 * np.pi * (np.outer(index, index) % N) / N
    cosine, sine = np.cos(angle), np.sin(angle)
    forward = np.block([[cosine, -sine], [sine, cosine]])

    def split(matrix):
        high = matrix.astype(np.float32).astype(ml_dtypes.bfloat16)
        low = (matrix - high.astype(np.float64)).astype(np.float32).astype(ml_dtypes.bfloat16)
        return high, low

    def right(matrix):
        high, low = split(matrix)
        return np.concatenate([high, high, low], axis=0)

    def left(matrix):
        high, low = split(matrix)
        return np.concatenate([high, high, low], axis=1)

    return np.stack([right(forward), right(forward.T)]), np.stack([left(forward.T), left(forward)])


def parts(value, axis):
    high = value.astype(jnp.bfloat16)
    low = (value - high.astype(jnp.float32)).astype(jnp.bfloat16)
    return jnp.concatenate([high, low, high], axis=axis)


def from_right(value, matrix):
    return jnp.dot(parts(value, 1), matrix, preferred_element_type=jnp.float32)


def from_left(matrix, value):
    return jnp.dot(matrix, parts(value, 0), preferred_element_type=jnp.float32)


def signed_square(index):
    signed = jnp.where(index <= N // 2, index, index - N)
    return (signed * signed).astype(jnp.float32)


def kernel(
    orb_in, rights_in, lefts_in, own, out,
    orb, rights, lefts, srcs, send_a, recv_b, back, recv_c, terms, summed, gathered, coulomb, folded, folded_in,
    in_sem, src_recv, src_send, a_recv, a_send, c_recv, c_send, t_recv, t_send, z_recv, z_send, x_recv, x_send,
):
    band = lax.axis_index("band")
    me = lax.axis_index("fft")
    z = band // 4
    x_hi = lax.rem(band // 2, 2)
    core = lax.rem(band, 2)
    x_lo = me // 4
    y = lax.rem(me, 4)
    even = lax.rem(z, 2) == 0
    root = jnp.logical_and(jnp.logical_and(even, x_hi == 0), core == 0)
    lead = core == 0

    loads = [
        pltpu.make_async_copy(src, dst, in_sem.at[i])
        for i, (src, dst) in enumerate(((orb_in, orb), (rights_in, rights), (lefts_in, lefts)))
    ]
    for load in loads:
        load.start()

    def device(z_at, x_hi_at, core_at):
        return {"band": z_at * 4 + x_hi_at * 2 + core_at, "fft": me}

    plus = device(lax.rem(z + 1, ZS), x_hi, core)
    minus = device(lax.rem(z + ZS - 1, ZS), x_hi, core)
    minus2 = device(lax.rem(z + ZS - 2, ZS), x_hi, core)
    sibling = device(z, x_hi, 1 - core)
    across = device(z, 1 - x_hi, core)

    def peer_index(step):
        d_lo, d_y = step // 4, lax.rem(step, 4)
        return lax.rem(x_lo + d_lo, 2) * 4 + lax.rem(y + d_y, 4)

    barrier = pltpu.get_barrier_semaphore()

    def signal(target):
        pl.semaphore_signal(barrier, inc=1, device_id=target, device_id_type=MESH)

    for step in range(1, 8):
        signal({"band": band, "fft": peer_index(step)})
    for step in range(1, ZS):
        signal(device(lax.rem(z + step, ZS), x_hi, core))
    signal(sibling)
    signal(across)
    signal(device(z, 1 - x_hi, 1 - core))
    def fill_coulomb(k, carry):
        row = lax.broadcasted_iota(jnp.int32, (N, N), 0)
        column = lax.broadcasted_iota(jnp.int32, (N, N), 1)
        middle = jnp.full((N, N), me * SLAB + k, jnp.int32)
        total = signed_square(row) + signed_square(middle) + signed_square(column)
        scale = CELL * CELL / np.pi / float(N) ** 3
        coulomb[k] = jnp.where(total > 0, scale / jnp.maximum(total, 1.0), 0.0)
        return carry

    lax.fori_loop(0, SLAB, fill_coulomb, 0)

    loads[0].wait()
    pl.semaphore_wait(barrier, 17)

    def round_of(slot):
        return lax.rem(z // 2 + slot, ROUNDS)

    def planes(j):
        return pl.ds(2 * j, 2)

    def remote(src, dst, send_sem, recv_sem, target):
        return pltpu.make_async_remote_copy(
            src_ref=src, dst_ref=dst, send_sem=send_sem, recv_sem=recv_sem, device_id=target, device_id_type=MESH
        )

    def pass_on(src, slot, j, kind, target):
        r = round_of(slot)
        remote(src, srcs.at[r, planes(j)], src_send.at[slot, kind], src_recv.at[r, j], target).start()

    def pass_early(chunk, j):
        @pl.when(j < EARLY)
        def _():
            pass_on(chunk, 0, j, 4, minus2)

    @pl.when(root)
    def _():
        def body(j, carry):
            chunk = orb.at[planes(j)]
            pass_on(chunk, 0, j, 3, across)
            pass_early(chunk, j)
            pass_on(chunk, 0, j, 1, minus)
            pass_on(chunk, 0, j, 0, plus)
            pass_on(chunk, 0, j, 2, sibling)
            return carry

        lax.fori_loop(0, STEPS, body, 0)

        def fill(j, carry):
            srcs[round_of(0), planes(j)] = orb[planes(j)]
            return carry

        lax.fori_loop(0, STEPS, fill, 0)

    def arrive(slot, j):
        r = round_of(slot)
        chunk = srcs.at[r, planes(j)]

        def take():
            pltpu.make_async_copy(chunk, chunk, src_recv.at[r, j]).wait()

            @pl.when(lead)
            def _():
                if slot == 1:

                    @pl.when(jnp.logical_or(even, j >= EARLY))
                    def _():
                        pass_on(chunk, slot, j, 1, minus)

                if slot == 0:

                    @pl.when(even)
                    def _():
                        pass_early(chunk, j)
                        pass_on(chunk, slot, j, 1, minus)

                if slot in (0, 3):
                    pass_on(chunk, slot, j, 0, plus)
                pass_on(chunk, slot, j, 2, sibling)

        if slot == 0:
            pl.when(jnp.logical_not(root))(take)
        else:
            take()

    for load in loads[1:]:
        load.wait()

    def left_fwd(p, j):
        blocks = send_a.at[p, pl.ds(0, 2), :, pl.ds(0, 7 * SLAB), :]
        pltpu.make_async_copy(blocks, blocks, a_send.at[p, j]).wait()

    def forward(p, j):
        r_a, r_b = round_of(2 * p), round_of(2 * p + 1)
        rows = []
        for i in range(2):
            o = orb[2 * j + i]
            rows.append(jnp.concatenate([o * srcs[r_a, 2 * j + i], o * srcs[r_b, 2 * j + i]], axis=1))
        along_z = from_right(jnp.concatenate(rows, axis=0), rights[0])
        real = jnp.concatenate([along_z[:N, :N], along_z[N:, :N]], axis=1)
        imag = jnp.concatenate([along_z[:N, N:], along_z[N:, N:]], axis=1)
        along_y = from_left(lefts[0], jnp.concatenate([real, imag], axis=0))
        for i in range(2):
            for part in range(2):
                send_a[p, 2 * j + i, part] = along_y[part * N : (part + 1) * N, i * N : (i + 1) * N]
        place = pl.ds(me * SLAB + 2 * j, 2)

        def block(f):
            return send_a.at[p, planes(j), :, pl.ds(pl.multiple_of(f * SLAB, SLAB), SLAB), :]

        if p > 0:
            pl.when(j < DEPTH)(lambda: left_fwd(p - 1, j + STEPS - DEPTH))
        pl.when(j >= DEPTH)(lambda: left_fwd(p, j - DEPTH))

        for step in (5, 7, 6, 1, 3, 2, 4):
            f = peer_index(step)
            remote(
                block(f), recv_b.at[p, place], a_send.at[p, j], a_recv.at[p], {"band": band, "fft": f}
            ).start()
        pltpu.make_async_copy(block(me), recv_b.at[p, place], a_recv.at[p]).start()

    behind = {0: 0, 1: jnp.where(even, LAG, 1), 3: jnp.where(even, 6, 9), 2: jnp.where(even, 11, 9)}

    def relay(i):
        for slot in (0, 1, 3, 2):
            j = i - behind[slot]

            @pl.when(jnp.logical_and(j >= 0, j < STEPS))
            def _():
                arrive(slot, j)

    def first_steps(i, carry):
        relay(i)

        @pl.when(i >= LAG)
        def _():
            forward(0, i - LAG)

        return carry

    def second_steps(i, carry):
        relay(i)
        forward(1, i - STEPS - LAG)
        return carry

    lax.fori_loop(0, STEPS + LAG, first_steps, 0)
    lax.fori_loop(STEPS + LAG, 2 * STEPS + LAG, second_steps, 0)

    def middle(p):
        pltpu.make_async_copy(recv_b.at[p], recv_b.at[p], a_recv.at[p]).wait()
        flat_in = recv_b.at[p].reshape(N * 2 * SLAB, N)
        flat_out = back.at[p].reshape(N * 2 * SLAB, N)

        def rows(part, k):
            return pl.ds(part * SLAB + k, N, stride=2 * SLAB)

        def body(i, carry):
            blocks = [
                jnp.concatenate([flat_in[rows(part, 2 * i), :], flat_in[rows(part, 2 * i + 1), :]], axis=1)
                for part in range(2)
            ]
            spectrum = from_left(lefts[0], jnp.concatenate(blocks, axis=0))
            weight = jnp.concatenate([coulomb[2 * i], coulomb[2 * i + 1]], axis=1)
            spectrum = spectrum * jnp.concatenate([weight, weight], axis=0)
            result = from_left(lefts[1], spectrum)
            for part in range(2):
                for n in range(2):
                    flat_out[rows(part, 2 * i + n), :] = result[part * N : (part + 1) * N, n * N : (n + 1) * N]
            return carry

        lax.fori_loop(0, SLAB // 2, body, 0)

        def give(j, carry):
            def place(ref):
                return ref.at[p, planes(j), :, pl.ds(pl.multiple_of(me * SLAB, SLAB), SLAB), :]

            for step in (5, 7, 6, 1, 3, 2, 4):
                f = peer_index(step)
                remote(
                    back.at[p, pl.ds(f * SLAB + 2 * j, 2)], place(recv_c), c_send.at[p], c_recv.at[p, j],
                    {"band": band, "fft": f},
                ).start()
            pltpu.make_async_copy(
                back.at[p, pl.ds(me * SLAB + 2 * j, 2)], place(recv_c), c_recv.at[p, j]
            ).start()
            return carry

        lax.fori_loop(0, STEPS, give, 0)

    for p in range(PACKS):
        middle(p)

    def inverse(p, j):
        chunk = recv_c.at[p, planes(j)]
        pltpu.make_async_copy(chunk, chunk, c_recv.at[p, j]).wait()
        parts_in = [
            jnp.concatenate([recv_c[p, 2 * j, part], recv_c[p, 2 * j + 1, part]], axis=1) for part in range(2)
        ]
        along_y = from_left(lefts[1], jnp.concatenate(parts_in, axis=0))
        rows = [
            jnp.concatenate([along_y[:N, i * N : (i + 1) * N], along_y[N:, i * N : (i + 1) * N]], axis=1)
            for i in range(2)
        ]
        potential = from_right(jnp.concatenate(rows, axis=0), rights[1])
        r_a, r_b = round_of(2 * p), round_of(2 * p + 1)
        for i in range(2):
            pot_a = potential[i * N : (i + 1) * N, :N]
            pot_b = potential[i * N : (i + 1) * N, N:]
            share = srcs[r_a, 2 * j + i] * pot_a + srcs[r_b, 2 * j + i] * pot_b
            if p > 0:
                share = own[2 * j + i] + share
            own[2 * j + i] = share
            o = orb[2 * j + i]
            terms[p, j, i, 0] = o * pot_a
            terms[p, j, i, 1] = o * pot_b
        remote(
            terms.at[p, j, 1 - core], summed.at[p, j], t_send.at[p], t_recv.at[p, j], sibling
        ).start()

    def spread(p, j):
        chunk = summed.at[p, j]
        pltpu.make_async_copy(chunk, chunk, t_recv.at[p, j]).wait()
        summed[p, j] = summed[p, j] + terms[p, j, core]

        def rows(z_at):
            return summed.at[p, j, :, pl.ds(pl.multiple_of(z_at * 16, 16), 16), :]

        for step in (4, 3, 5, 2, 6, 1, 7):
            z_at = lax.rem(z + step, ZS)
            remote(
                rows(z_at), gathered.at[z, pl.ds(2 * p, 2), j], z_send.at[p], z_recv.at[j], device(z_at, x_hi, core)
            ).start()
        gathered[z, pl.ds(2 * p, 2), j] = summed[p, j, :, pl.ds(pl.multiple_of(z * 16, 16), 16), :]

    others = (
        (1 - x_hi, core, across), (x_hi, 1 - core, sibling), (1 - x_hi, 1 - core, device(z, 1 - x_hi, 1 - core)),
    )

    def last(j, n):
        x_hi_at, core_at, target = others[n]
        return remote(
            folded.at[j, x_hi_at, core_at], folded_in.at[n, j], x_send.at[n], x_recv.at[n, j], target
        )

    def fold(j):
        arrived = gathered.at[pl.ds(0, 7), :, j]
        pltpu.make_async_copy(arrived, arrived, z_recv.at[j]).wait()
        totals = []
        for r in range(ROUNDS):
            total = gathered[0, r, j]
            for z_at in range(1, ZS):
                total = total + gathered[z_at, (r - z_at // 2) % ROUNDS, j]
            totals.append(total)
        for x_hi_at in range(2):
            for core_at in range(2):
                for n in range(2):
                    rows = slice(8 * x_hi_at + 4 * core_at, 8 * x_hi_at + 4 * core_at + 4)
                    folded[j, x_hi_at, core_at, n] = jnp.concatenate(
                        [totals[2 * n][rows], totals[2 * n + 1][rows]], axis=0
                    )
        for n in range(3):
            last(j, n).start()

    def write(j):
        for n in range(3):
            last(j, n).wait_recv()
        mine = folded[j, x_hi, core] + folded_in[0, j]
        theirs = folded_in[1, j] + folded_in[2, j]
        for r in range(ROUNDS):
            rows = slice(4 * (r % 2), 4 * (r % 2) + 4)
            out[r, 2 * j + core] = mine[r // 2, rows]
            out[r, 2 * j + 1 - core] = theirs[r // 2, rows]

    def second_half(p, stages, i, carry):
        for late, stage in stages:
            j = i - late

            @pl.when(jnp.logical_and(j >= 0, j < STEPS))
            def _():
                stage(j)

        return carry

    for p in range(PACKS):
        stages = [(0, functools.partial(inverse, p)), (1, functools.partial(spread, p))]
        if p == PACKS - 1:
            stages += [(3, fold), (5, write)]
        lax.fori_loop(0, STEPS + stages[-1][0], functools.partial(second_half, p, stages), 0)

    for j in range(STEPS - DEPTH, STEPS):
        left_fwd(PACKS - 1, j)

    def sent(ref, sem):
        pltpu.make_async_copy(ref, ref, sem).wait()

    for p in range(PACKS):
        sent(back.at[p, pl.ds(0, 112)], c_send.at[p])
        sent(summed.at[p], t_send.at[p])
        sent(summed.at[p, pl.ds(0, 7)], z_send.at[p])
    for n in range(3):
        sent(folded_in.at[n], x_send.at[n])

    @pl.when(lead)
    def _():
        for slot, kind in ((0, 0), (0, 2), (1, 2), (2, 2), (3, 0), (3, 2)):
            sent(srcs.at[slot], src_send.at[slot, kind])

        @pl.when(even)
        def _():
            sent(srcs.at[0], src_send.at[0, 1])
            sent(srcs.at[1], src_send.at[1, 1])
            sent(srcs.at[0, pl.ds(0, 2 * EARLY)], src_send.at[0, 4])

        @pl.when(jnp.logical_not(even))
        def _():
            sent(srcs.at[1, pl.ds(2 * EARLY, SLAB - 2 * EARLY)], src_send.at[1, 1])

        @pl.when(root)
        def _():
            sent(srcs.at[0], src_send.at[0, 3])


def local(rights, lefts, orbitals):
    f32 = jnp.float32
    dma = pltpu.SemaphoreType.DMA
    vmem = pl.BlockSpec(memory_space=pltpu.VMEM)
    own, source = pl.pallas_call(
        kernel,
        out_shape=(
            jax.ShapeDtypeStruct((SLAB, N, N), f32),
            jax.ShapeDtypeStruct((ROUNDS, SLAB, 4, N), f32),
        ),
        in_specs=[pl.BlockSpec(memory_space=pltpu.HBM)] * 3,
        out_specs=(vmem, vmem),
        scratch_shapes=[
            pltpu.VMEM((SLAB, N, N), f32),
            pltpu.VMEM(rights.shape, rights.dtype),
            pltpu.VMEM(lefts.shape, lefts.dtype),
            pltpu.VMEM((ROUNDS, SLAB, N, N), f32),
            pltpu.VMEM((PACKS, SLAB, 2, N, N), f32),
            pltpu.VMEM((PACKS, N, 2, SLAB, N), f32),
            pltpu.VMEM((PACKS, N, 2, SLAB, N), f32),
            pltpu.VMEM((PACKS, SLAB, 2, N, N), f32),
            pltpu.VMEM((PACKS, STEPS, 2, 2, N, N), f32),
            pltpu.VMEM((PACKS, STEPS, 2, N, N), f32),
            pltpu.VMEM((ZS, ROUNDS, STEPS, 16, N), f32),
            pltpu.VMEM((SLAB, N, N), f32),
            pltpu.VMEM((STEPS, 2, 2, 2, 8, N), f32),
            pltpu.VMEM((3, STEPS, 2, 8, N), f32),
            dma((3,)),
            dma((ROUNDS, STEPS)),
            dma((ROUNDS, 5)),
            dma((PACKS,)),
            dma((PACKS, STEPS)),
            dma((PACKS, STEPS)),
            dma((PACKS,)),
            dma((PACKS, STEPS)),
            dma((PACKS,)),
            dma((STEPS,)),
            dma((PACKS,)),
            dma((3, STEPS)),
            dma((3,)),
        ],
        compiler_params=pltpu.CompilerParams(
            collective_id=0, has_side_effects=True, vmem_limit_bytes=56 * 2**20
        ),
        name="exchange",
    )(orbitals[0], rights, lefts)
    return own[None], source


def solution(mesh):
    tables = [jnp.asarray(table) for table in matrices()]
    in_specs = (P("band", "fft", None, None),)
    out_specs = (P("band", "fft", None, None), P(None, "fft", "band", None))
    body = functools.partial(local, *tables)
    return jax.shard_map(body, mesh=mesh, in_specs=in_specs, out_specs=out_specs, check_vma=False)
```
